128 devices in a mesh: dp: 2 (over core), expert: 64 (over y, x, z).
Axes of the slice: x: 4, y: 4, z: 4, core: 2. Of those that a mesh axis runs over, the one named last changes fastest.
Arguments:
- queries: bfloat16 [32768, 1280], P(('dp', 'expert')), may hold values from -28 to 28
- keys_in: bfloat16 [32768, 1280], P(('dp', 'expert')), may hold values from -16 to 16
- values_in: bfloat16 [32768, 1280], P(('dp', 'expert')), may hold values from -6 to 6
- resid: bfloat16 [32768, 1280], P(('dp', 'expert')), may hold values from -6 to 6
- out_proj: bfloat16 [1280, 1280], replicated, may hold values from -0.15625 to 0.15625
- ln_gain: float32 [1280], replicated, may hold values from 0.25 to 1.75
- w_in: bfloat16 [64, 1280, 2560], P('expert', None, 'dp'), may hold values from -0.15625 to 0.15625
- w_out: bfloat16 [64, 2560, 1280], P('expert', 'dp'), may hold values from -0.125 to 0.125
- route: int32 [4, 32768], P(None, ('dp', 'expert')), may hold values from 0 to 15, as said below
- slot: int32 [4, 32768], P(None, ('dp', 'expert')), may hold values from 0 to 8, as said below
- gates: float32 [4, 32768], P(None, ('dp', 'expert')), may hold values from 0.3 to 1
- cotangent: bfloat16 [4, 32768, 1280], P(None, ('dp', 'expert')), may hold values from -24 to 24
Outputs:
- resid_grad: bfloat16 [32768, 1280], P(('dp', 'expert'))
- query_grad: bfloat16 [32768, 1280], P(('dp', 'expert'))
- key_grad: bfloat16 [32768, 1280], P(('dp', 'expert'))
- value_grad: bfloat16 [32768, 1280], P(('dp', 'expert'))
- proj_grad: float32 [1280, 1280], P(None, ('dp', 'expert'))
- gain_grad: float32 [1280], P(('dp', 'expert'))
- gate_grad: float32 [4, 32768], P(None, ('dp', 'expert'))
- w_in_grad: bfloat16 [64, 1280, 2560], P('expert', None, 'dp')
- w_out_grad: bfloat16 [64, 2560, 1280], P('expert', 'dp')
The draws below stay inside these ranges and needn't reach their ends.
Inputs may be any that keep to these rules, and one draw needn't show every extreme that they name: route[m, t] names one of the 16 experts of member m. slot[m, t] == 8 marks a dropped token; among the tokens of one device that member m sends to one expert, the kept ones have distinct slots.
All inputs are finite; a program needn't handle non-finite values.
Results may differ from the reference program's by a relative error of at most 0.025.
Values may be sent and summed in bfloat16 or wider, within the bound.
A program may use at most 128 MiB of HBM per device.

```python
import math
import jax
import jax.numpy as jnp
from jax import lax

D = 1280
HEADS = 16
HEAD = 80
H = 2560
MEMBERS = 4
SEQ = 256
TOK_DEV = 256
CAP = 8
EXPERTS = 64
TOKENS = 32768
N_DP = 2


def routing(key):
    devices = TOKENS // TOK_DEV
    per_member = EXPERTS // MEMBERS
    shape = (MEMBERS, devices, TOK_DEV)
    favored = jax.random.randint(jax.random.fold_in(key, 101), (MEMBERS, 1, 1), 0, per_member)
    offsets = jax.random.randint(jax.random.fold_in(key, 102), (MEMBERS, devices, 1), 0, per_member)
    first_pick = jax.random.randint(jax.random.fold_in(key, 103), shape, 0, per_member)
    second_pick = jax.random.randint(jax.random.fold_in(key, 104), shape, 0, per_member)
    skewed = first_pick * second_pick // per_member
    position = jnp.arange(TOK_DEV, dtype=jnp.int32)
    leading = position < 2 * CAP
    base_route = jnp.where(leading, favored, (skewed + offsets) % per_member).astype(jnp.int32)
    order_keys = jax.random.randint(jax.random.fold_in(key, 105), shape, 0, 4096) * TOK_DEV + position
    order = jnp.argsort(order_keys, axis=-1)
    routed = jnp.take_along_axis(base_route, order, axis=-1)
    priority = jax.random.randint(jax.random.fold_in(key, 106), shape, 0, 4096) * TOK_DEV + position
    same_expert = routed[..., :, None] == routed[..., None, :]
    earlier = priority[..., None, :] < priority[..., :, None]
    ranking = jnp.sum(same_expert & earlier, axis=-1).astype(jnp.int32)
    slots = jnp.minimum(ranking, CAP).astype(jnp.int32)
    return (routed.reshape(MEMBERS, TOKENS).astype(jnp.int32), slots.reshape(MEMBERS, TOKENS))


def draw_route(key, part):
    shared = routing(key)
    return shared[0]


def draw_slot(key, part):
    shared = routing(key)
    return shared[1]


def key_base(key):
    return jnp.clip(jax.random.normal(key, (TOKENS, D), jnp.float32), -4.0, 4.0)


def draw_keys_in(key, part):
    base = key_base(key)
    return base.astype(jnp.bfloat16)


def draw_queries(key, part):
    key = jax.random.fold_in(key, 22)
    fresh = jnp.clip(jax.random.normal(key, (TOKENS, D), jnp.float32), -4.0, 4.0)
    return fresh.astype(jnp.bfloat16)


def with_spikes(entries, rng, source, target, shards_of, factor):
    def block_of(dim):
        return (jnp.arange(entries.shape[dim]) // (entries.shape[dim] // shards_of)).reshape((-1,) + (1,) * (entries.ndim - 1 - dim))

    one_side = jax.random.permutation(rng, shards_of)[block_of(target)]
    far = (block_of(target) + shards_of // 2) % shards_of
    return jnp.where((block_of(source) == one_side) | (block_of(source) == far), factor * entries, entries)


def steps_of(stream_key, shape, split, smallest, high):
    loudness, own = 1.0, jax.random.fold_in(stream_key, 6)
    for dim, blocks in split:
        draws = jnp.exp(jax.random.uniform(jax.random.fold_in(own, dim), (blocks,), jnp.float32, smallest / len(split), high / len(split)))
        loudness = loudness * jnp.repeat(draws, shape[dim] // blocks).reshape([-1 if axis == dim else 1 for axis in range(len(shape))])
    return loudness


def scatter_about(stream_key, extent, width, bound, cuts=(), kind=jnp.bfloat16):
    drawn = width * jax.random.normal(stream_key, extent, jnp.float32)
    if cuts:
        drawn = drawn * steps_of(stream_key, extent, cuts, -0.22, 0.18)
    return jnp.clip(drawn, -bound, bound).astype(kind)


def gaussian_with(key, extent, width, bound, shards, heavy, kind=jnp.bfloat16):
    values = width * jax.random.normal(key, extent, jnp.float32)
    if shards:
        values = values * steps_of(key, extent, shards, -0.22, 0.18)
    return jnp.clip(with_spikes(values, jax.random.fold_in(key, 3), *heavy), -bound, bound).astype(kind)


def setup_inputs(seed: int = 0) -> dict:
    key_of = jax.random.split(jax.random.key(seed), 13)
    queries = draw_queries(jax.random.fold_in(key_of[12], 71), 0)
    keys_in = draw_keys_in(jax.random.fold_in(key_of[12], 71), 0)
    values_in = scatter_about(key_of[2], (TOKENS, D), 1.0, 6.0, ((0, 128),))
    resid = scatter_about(key_of[3], (TOKENS, D), 1.0, 6.0, ((0, 128),))
    out_proj = scatter_about(key_of[4], (D, D), D ** -0.5, 0.15625)
    ln_gain = jnp.clip(1.0 + 0.15 * jax.random.normal(key_of[5], (D,), jnp.float32), 0.25, 1.75)
    w_in = scatter_about(key_of[6], (EXPERTS, D, H), D ** -0.5, 0.15625, ((0, 64), (2, 2)))
    w_out = scatter_about(key_of[7], (EXPERTS, H, D), H ** -0.5, 0.125, ((0, 64), (1, 2)))
    route = draw_route(jax.random.fold_in(key_of[12], 71), 0)
    slot = draw_slot(jax.random.fold_in(key_of[12], 71), 0)
    gates = jnp.clip(0.3 + 0.7 * jax.random.uniform(key_of[10], (MEMBERS, TOKENS), jnp.float32) ** steps_of(key_of[10], (MEMBERS, TOKENS), ((1, 128),), -0.2, 0.2), 0.3, 1.0)
    cotangent = gaussian_with(key_of[11], (MEMBERS, TOKENS, D), 1.0, 24.0, ((1, 128),), (1, 2, 128, 5.5))
    return {"queries": queries, "keys_in": keys_in, "values_in": values_in, "resid": resid, "out_proj": out_proj, "ln_gain": ln_gain, "w_in": w_in, "w_out": w_out, "route": route, "slot": slot, "gates": gates, "cotangent": cotangent}


epsilon = 1e-06

def gelu_exact(values):
    return jax.nn.gelu(values, approximate=False)

def attend(query_rows, key_rows, value_rows):
    images = query_rows.shape[0] // SEQ
    shaped = (images, SEQ, HEADS, HEAD)
    query_heads = query_rows.astype(jnp.float32).reshape(shaped)
    key_heads = key_rows.astype(jnp.float32).reshape(shaped)
    value_heads = value_rows.astype(jnp.float32).reshape(shaped)
    scores = jnp.einsum('bqhd,bkhd->bhqk', query_heads, key_heads) / math.sqrt(HEAD)
    weights = jax.nn.softmax(scores, axis=-1).astype(jnp.bfloat16).astype(jnp.float32)
    mixed_heads = jnp.einsum('bhqk,bkhd->bqhd', weights, value_heads)
    return mixed_heads.reshape(query_rows.shape).astype(jnp.bfloat16)

def attend_grads(packed):
    query_rows, key_rows, value_rows, upstream = packed
    _, attend_back = jax.vjp(attend, query_rows, key_rows, value_rows)
    return attend_back(upstream)

def attend_block(packed):
    return attend(packed[0], packed[1], packed[2])

def normed(stream_f, gain):
    average = lax.optimization_barrier(jnp.mean(stream_f, axis=-1, keepdims=True))
    centred = stream_f - average
    spread_sq = lax.optimization_barrier(jnp.mean(centred * centred, axis=-1, keepdims=True))
    return centred * lax.rsqrt(spread_sq + epsilon) * gain

def halves(left, right):
    half_width = right.shape[0] // N_DP
    split_left = left.astype(jnp.float32).reshape(left.shape[0], N_DP, half_width)
    split_right = right.astype(jnp.float32).reshape(N_DP, half_width, right.shape[1])
    partials = jnp.einsum('rkh,khd->krd', split_left, split_right).astype(jnp.bfloat16).astype(jnp.float32)
    return lax.optimization_barrier(jnp.sum(partials, axis=0)).astype(jnp.bfloat16)

def expert_step(packed):
    in_rows, grad_rows, first, second = packed
    pre_act = jnp.dot(in_rows, first, preferred_element_type=jnp.float32)
    hidden = gelu_exact(pre_act).astype(jnp.bfloat16)
    expert_out = halves(hidden, second)
    d_hidden = jnp.dot(grad_rows, second.T, preferred_element_type=jnp.float32)
    _, gelu_back = jax.vjp(gelu_exact, pre_act)
    d_pre = gelu_back(d_hidden)[0].astype(jnp.bfloat16)
    w_out_grad = jnp.dot(hidden.T, grad_rows, preferred_element_type=jnp.float32).astype(jnp.bfloat16)
    w_in_grad = jnp.dot(in_rows.T, d_pre, preferred_element_type=jnp.float32).astype(jnp.bfloat16)
    back_rows = halves(d_pre, first.T)
    return (expert_out, back_rows, w_in_grad, w_out_grad)

def pick(buffer, flat_index, kept_mask):
    row_limit = buffer.shape[0] - 1
    picked_rows = buffer[jnp.minimum(flat_index, row_limit)].astype(jnp.float32)
    return jnp.where(kept_mask[..., None], picked_rows, 0.0)

def reference(queries, keys_in, values_in, resid, out_proj, ln_gain, w_in, w_out, route, slot, gates, cotangent):
    devices = TOKENS // TOK_DEV
    per_member = EXPERTS // MEMBERS

    def blocks(array):
        return array.reshape((devices, TOK_DEV) + array.shape[1:])
    mixed_heads = lax.map(attend_block, (blocks(queries), blocks(keys_in), blocks(values_in))).reshape(TOKENS, D)
    stream = (resid.astype(jnp.float32) + jnp.dot(mixed_heads, out_proj, preferred_element_type=jnp.float32)).astype(jnp.bfloat16)
    normed_f, norm_back = jax.vjp(normed, stream.astype(jnp.float32), ln_gain)
    entering = normed_f.astype(jnp.bfloat16)
    source = (jnp.arange(TOKENS, dtype=jnp.int32) // TOK_DEV).astype(jnp.int32)
    expert_ids = route + per_member * jnp.arange(MEMBERS, dtype=jnp.int32)[:, None]
    kept_mask = slot < CAP
    rows_each = devices * CAP
    flat_index = jnp.where(kept_mask, expert_ids * rows_each + source[None, :] * CAP + slot, EXPERTS * rows_each).astype(jnp.int32)
    tiled_rows = jnp.broadcast_to(entering[None], (MEMBERS, TOKENS, D)).reshape(-1, D)
    forward_buffer = jnp.zeros((EXPERTS * rows_each, D), jnp.bfloat16).at[flat_index.reshape(-1)].set(tiled_rows, mode='drop')
    cot_f = cotangent.astype(jnp.float32)
    scaled = (gates[..., None] * cot_f).astype(jnp.bfloat16)
    grad_buffer = jnp.zeros((EXPERTS * rows_each, D), jnp.bfloat16).at[flat_index.reshape(-1)].set(scaled.reshape(-1, D), mode='drop')
    shape3 = (EXPERTS, rows_each, D)
    expert_out, back_rows, w_in_grad, w_out_grad = lax.map(expert_step, (forward_buffer.reshape(shape3), grad_buffer.reshape(shape3), w_in, w_out))
    outputs = pick(expert_out.reshape(-1, D), flat_index, kept_mask)
    gate_grad = lax.optimization_barrier(jnp.sum(cot_f * outputs, axis=-1))
    d_norm = lax.optimization_barrier(jnp.sum(pick(back_rows.reshape(-1, D), flat_index, kept_mask), axis=0))
    d_stream, gain_grad = norm_back(d_norm)
    resid_grad = (lax.optimization_barrier(jnp.sum(cot_f, axis=0)) + d_stream).astype(jnp.bfloat16)
    proj_grad = jnp.dot(mixed_heads.T, resid_grad, preferred_element_type=jnp.float32)
    d_mixed = jnp.dot(resid_grad, out_proj.T, preferred_element_type=jnp.float32).astype(jnp.bfloat16)
    query_grad, key_grad, value_grad = lax.map(attend_grads, (blocks(queries), blocks(keys_in), blocks(values_in), blocks(d_mixed)))
    return (resid_grad, query_grad.reshape(TOKENS, D), key_grad.reshape(TOKENS, D), value_grad.reshape(TOKENS, D), proj_grad, gain_grad, gate_grad, w_in_grad, w_out_grad)
```

```python
import math

import jax
import jax.numpy as jnp
from jax import lax
from jax.sharding import PartitionSpec as P

HEADS = 16
HEAD = 80
SEQ = 256
CAP = 8


epsilon = 1e-06


def gelu_exact(values):
    return jax.nn.gelu(values, approximate=False)


def attend(query_rows, key_rows, value_rows):
    images = query_rows.shape[0] // SEQ
    shaped = (images, SEQ, HEADS, HEAD)
    query_heads = query_rows.astype(jnp.float32).reshape(shaped)
    key_heads = key_rows.astype(jnp.float32).reshape(shaped)
    value_heads = value_rows.astype(jnp.float32).reshape(shaped)
    scores = jnp.einsum("bqhd,bkhd->bhqk", query_heads, key_heads) / math.sqrt(HEAD)
    weights = jax.nn.softmax(scores, axis=-1).astype(jnp.bfloat16).astype(jnp.float32)
    mixed_heads = jnp.einsum("bhqk,bkhd->bqhd", weights, value_heads)
    return mixed_heads.reshape(query_rows.shape).astype(jnp.bfloat16)


def normed(stream_f, gain):
    average = jnp.mean(stream_f, axis=-1, keepdims=True)
    centred = stream_f - average
    spread_sq = jnp.mean(centred * centred, axis=-1, keepdims=True)
    return centred * lax.rsqrt(spread_sq + epsilon) * gain


def selection(route, slot, n_exp):
    per_member = n_exp // route.shape[0]
    row = jnp.where(slot < CAP, route * CAP + slot, -1)
    rows = lax.broadcasted_iota(jnp.int32, (1, per_member * CAP, 1), 1)
    return rows == row[:, None, :]


def to_expert(buffer):
    arrived = lax.all_to_all(buffer, "expert", split_axis=0, concat_axis=0, tiled=True)
    return lax.all_gather(arrived, "dp", axis=0, tiled=True)


def to_tokens(partial_sums):
    mine = lax.psum_scatter(
        partial_sums.astype(jnp.bfloat16), "dp", scatter_dimension=0, tiled=True
    )
    return lax.all_to_all(mine, "expert", split_axis=0, concat_axis=0, tiled=True)


def shards(
    queries,
    keys_in,
    values_in,
    resid,
    out_proj,
    ln_gain,
    w_in,
    w_out,
    route,
    slot,
    gates,
    cotangent,
):
    n_exp = lax.axis_size("expert")
    mixed_heads = attend(queries, keys_in, values_in)
    stream = (
        resid.astype(jnp.float32)
        + jnp.dot(mixed_heads, out_proj, preferred_element_type=jnp.float32)
    ).astype(jnp.bfloat16)
    normed_f, norm_back = jax.vjp(normed, stream.astype(jnp.float32), ln_gain)
    entering = normed_f.astype(jnp.bfloat16)
    one_hot = selection(route, slot, n_exp).astype(jnp.bfloat16)
    width = entering.shape[-1]
    cot_f = cotangent.astype(jnp.float32)
    scaled = (gates[..., None] * cot_f).astype(jnp.bfloat16)
    grad_rows = jnp.einsum("mrt,mtd->mrd", one_hot, scaled)
    grad_rows = to_expert(grad_rows.reshape(n_exp, CAP, width)).reshape(-1, width)
    expert_rows = jnp.einsum("mrt,td->mrd", one_hot, entering)
    expert_rows = to_expert(expert_rows.reshape(n_exp, CAP, width)).reshape(-1, width)
    w_first = w_in[0]
    w_second = w_out[0]
    d_hidden = jnp.dot(grad_rows, w_second.T, preferred_element_type=jnp.float32)
    pre_act = jnp.dot(expert_rows, w_first, preferred_element_type=jnp.float32)
    hidden_f, gelu_back = jax.vjp(gelu_exact, pre_act)
    hidden = hidden_f.astype(jnp.bfloat16)
    gate_dot = jnp.sum(hidden.astype(jnp.float32) * d_hidden, axis=-1, keepdims=True)
    d_pre = gelu_back(d_hidden)[0].astype(jnp.bfloat16)
    back = jnp.dot(d_pre, w_first.T, preferred_element_type=jnp.float32)
    back = jnp.concatenate([back, jnp.broadcast_to(gate_dot, (back.shape[0], 128))], axis=1)
    back = to_tokens(back.reshape(-1, CAP, width + 128)).reshape(one_hot.shape[:2] + (width + 128,))
    w_out_grad = jnp.dot(hidden.T, grad_rows, preferred_element_type=jnp.float32).astype(
        jnp.bfloat16
    )[None]
    w_in_grad = jnp.dot(expert_rows.T, d_pre, preferred_element_type=jnp.float32).astype(
        jnp.bfloat16
    )[None]
    gate_rows = back[:, :, width].astype(jnp.float32)
    gate_grad = jnp.sum(jnp.where(one_hot > 0, gate_rows[:, :, None], 0.0), axis=1) / gates
    d_norm = jnp.einsum(
        "mrt,mrd->td", one_hot, back[:, :, :width], preferred_element_type=jnp.float32
    )
    d_stream, gain_local = norm_back(d_norm)
    resid_grad = (jnp.sum(cot_f, axis=0) + d_stream).astype(jnp.bfloat16)
    proj_term = jnp.dot(resid_grad.T, mixed_heads, preferred_element_type=jnp.float32)
    n_dev = 2 * n_exp
    share = width // n_dev
    gain_part = jnp.pad(gain_local.reshape(n_dev, 1, share), ((0, 0), (0, 0), (0, width - share)))
    both = jnp.concatenate([proj_term.reshape(n_dev, share, width), gain_part], axis=1)
    both = lax.psum_scatter(both.astype(jnp.bfloat16), "dp", scatter_dimension=0, tiled=True)
    both = lax.all_to_all(both, "expert", split_axis=0, concat_axis=0, tiled=True)
    both = jnp.sum(both.astype(jnp.float32), axis=0)
    proj_grad, gain_grad = both[:share].T, both[share, :share]
    d_mixed = jnp.dot(resid_grad, out_proj.T, preferred_element_type=jnp.float32).astype(
        jnp.bfloat16
    )
    _, attend_back = jax.vjp(attend, queries, keys_in, values_in)
    query_grad, key_grad, value_grad = attend_back(d_mixed)
    return (
        resid_grad,
        query_grad,
        key_grad,
        value_grad,
        proj_grad,
        gain_grad,
        gate_grad,
        w_in_grad,
        w_out_grad,
    )


def solution(mesh):
    return jax.shard_map(
        shards,
        mesh=mesh,
        in_specs=(
            P(("dp", "expert"), None),
            P(("dp", "expert"), None),
            P(("dp", "expert"), None),
            P(("dp", "expert"), None),
            P(),
            P(),
            P("expert", None, "dp"),
            P("expert", "dp", None),
            P(None, ("dp", "expert")),
            P(None, ("dp", "expert")),
            P(None, ("dp", "expert")),
            P(None, ("dp", "expert"), None),
        ),
        out_specs=(
            P(("dp", "expert"), None),
            P(("dp", "expert"), None),
            P(("dp", "expert"), None),
            P(("dp", "expert"), None),
            P(None, ("dp", "expert")),
            P(("dp", "expert")),
            P(None, ("dp", "expert")),
            P("expert", None, "dp"),
            P("expert", "dp", None),
        ),
        check_vma=False,
    )
```

```python
import functools
import math

import jax
import jax.numpy as jnp
import numpy as np
from jax import lax
from jax.experimental import pallas as pl
from jax.experimental.pallas import tpu as pltpu
from jax.sharding import PartitionSpec as P

D = 1280
HALF = 640
HEADS = 16
HEAD = 80
TOK = 256
MEMBERS = 4
CAP = 8
CHIPS = 64
ROWS = CHIPS * CAP
BLOCK = 256
H = 2560
LANES = 512
SHARE = 10
EPS = 1e-06
MESH = pl.DeviceIdType.MESH
F32 = jnp.float32
BF16 = jnp.bfloat16


def product(a, b, contract):
    return lax.dot_general(a, b, (((contract[0],), (contract[1],)), ((), ())), preferred_element_type=F32)


def nn(a, b):
    return product(a, b, (1, 0))


def nt(a, b):
    return product(a, b, (1, 1))


def tn(a, b):
    return product(a, b, (0, 0))


def two_lanes(ref, n, *lead):
    low = pl.multiple_of(n * 128, 128)
    high = pl.multiple_of(HALF + n * 128, 128)
    return jnp.concatenate([ref[(*lead, slice(None), pl.ds(low, 128))], ref[(*lead, slice(None), pl.ds(high, 128))]], axis=1)


def pack(rows):
    count = rows.shape[0] // CAP
    low = rows[:, :128].reshape(count, CAP, 128)
    high = rows[:, 128:].reshape(count, CAP, 128)
    return jnp.concatenate([low, high], axis=1).astype(BF16)


def gelu_with_grad(x):
    u = 1.0 / (1.0 + (0.3275911 * math.sqrt(0.5)) * jnp.abs(x))
    poly = u * (0.254829592 + u * (-0.284496736 + u * (1.421413741 + u * (-1.453152027 + u * 1.061405429))))
    e = jnp.exp(-0.5 * x * x)
    tail = 0.5 * poly * e
    cdf = jnp.where(x >= 0.0, 1.0 - tail, tail)
    return x * cdf, cdf + x * (e * (1.0 / math.sqrt(2.0 * math.pi)))


def block_orders():
    d = np.arange(HALF)
    y, x, z, r = d // 160, (d // 40) % 4, (d // 10) % 4, d % 10
    out = np.zeros((2, HALF, HALF), np.float32)
    out[0, d, x * 160 + y * 40 + z * 10 + r] = 1.0
    out[1, d, z * 160 + y * 40 + x * 10 + r] = 1.0
    return out


def kernel(
    q_in, k_in, v_in, res_in, proj_in, gain_ref, first_in, second_in, route_ref, slot_ref, gates_ref, cot_in, order_in,
    resid_out, q_out, k_out, v_out, share_out, gate_out, first_out, second_out,
    q_v, k_v, v_v, res_v, proj_v, cot_v, order_v, first_v, second_v,
    attn_v, acc_v, mixed_v, mixed_p, rstd_v, enter_v, pick_v,
    send_a, send_b, grad_recv, enter_recv, back_recv,
    grad_v, enter_rows, grad_p, enter_p, hidden_v, dpre_v, hidden_p, dpre_p, dot_v,
    rg_v, rg_p, perm_v, resid_v, dmix_v, gate_send, gate_recv,
    sum1, recv1, sum2, recv2, sum3, recv3,
    load_sem, store_sem, local_sem, pair_send, pair_recv, a2a_send, a2a_recv, rs_send, rs_recv,
):
    core = lax.axis_index("dp")
    chip = lax.axis_index("expert")
    place = (chip // 16, (chip // 4) % 4, chip % 4)

    def offsets(n):
        q = n // 16
        return ((q % 2) * 2 + q // 2, (n // 4) % 4, n % 4)

    def ahead(n):
        o = offsets(n)
        return ((place[0] + o[0]) % 4) * 16 + ((place[1] + o[1]) % 4) * 4 + (place[2] + o[2]) % 4

    def behind(n):
        o = offsets(n)
        return ((place[0] + 4 - o[0]) % 4) * 16 + ((place[1] + 4 - o[1]) % 4) * 4 + (place[2] + 4 - o[2]) % 4

    def load(n, src, dst):
        return pltpu.make_async_copy(src, dst, load_sem.at[n])

    loads = [
        load(0, cot_in, cot_v),
        load(1, q_in, q_v),
        load(2, k_in, k_v),
        load(3, v_in, v_v),
        load(4, proj_in, proj_v),
        load(5, res_in, res_v),
        load(6, second_in.at[0], second_v.at[pl.ds(0, D)]),
        load(7, first_in.at[0], first_v.at[:, pl.ds(0, D)]),
        load(8, order_in, order_v),
    ]
    for item in loads:
        item.start()

    barrier = pltpu.get_barrier_semaphore()

    @pl.loop(1, CHIPS)
    def _(n):
        pl.semaphore_signal(barrier, inc=1, device_id=(core, ahead(n)), device_id_type=MESH)

    pl.semaphore_signal(barrier, inc=1, device_id=(1 - core, chip), device_id_type=MESH)

    def pair(n, src, dst):
        return pltpu.make_async_remote_copy(
            src, dst, pair_send.at[n], pair_recv.at[n], device_id=(1 - core, chip), device_id_type=MESH
        )

    row_iota = lax.broadcasted_iota(jnp.int32, (MEMBERS * 32, TOK), 0)
    row_of = jnp.where(slot_ref[...] < CAP, route_ref[...] * CAP + slot_ref[...], -1)
    loads[0].wait()
    for m in range(MEMBERS):
        picked = jnp.where(row_iota == row_of[m : m + 1, :], 1.0, 0.0)
        pick_v[m * 128 : (m + 1) * 128, :] = picked.astype(BF16)
        gate_rows = jnp.sum(picked * gates_ref[m : m + 1, :], axis=1, keepdims=True)

        @pl.loop(0, 5)
        def _(n, m=m, gate_rows=gate_rows):
            rows = nn(pick_v[m * 128 : (m + 1) * 128, :], two_lanes(cot_v, n, m)) * gate_rows
            send_a[m * 16 : (m + 1) * 16, :, pl.ds(pl.multiple_of(n * 128, 128), 128)] = pack(rows)

    pl.semaphore_wait(barrier, CHIPS)

    pair_second = pair(0, second_in.at[0], second_v.at[pl.ds(D, D)])
    pair_first = pair(1, first_in.at[0], first_v.at[:, pl.ds(D, D)])
    pair_second.start()
    pair_first.start()

    def dispatch(which, src, dst):
        own = pltpu.make_async_copy(src.at[chip], dst.at[0], local_sem.at[which])
        own.start()

        @pl.loop(1, CHIPS)
        def _(n):
            to = ahead(n)
            pltpu.make_async_remote_copy(
                src.at[to], dst.at[n], a2a_send.at[which], a2a_recv.at[which * 2 + n // 32],
                device_id=(core, to), device_id_type=MESH,
            ).start()

        return own

    def wait_sent(which, ref, count):
        pltpu.make_async_remote_copy(
            ref.at[pl.ds(0, count)], ref.at[pl.ds(0, count)], a2a_send.at[which], a2a_recv.at[which * 2],
            device_id=(1 - core, chip), device_id_type=MESH,
        ).wait_send()

    def wait_landed(n, ref, start, count):
        pltpu.make_async_remote_copy(
            ref.at[pl.ds(start, count)], ref.at[pl.ds(start, count)], a2a_send.at[0], a2a_recv.at[n],
            device_id=(1 - core, chip), device_id_type=MESH,
        ).wait_recv()

    own_grad = dispatch(0, send_a, grad_recv)

    def head_window(h):
        tile = (h * HEAD) // 128
        tile = tile - tile // 9
        lanes = lax.broadcasted_iota(jnp.int32, (1, 256), 1)
        first = h * HEAD - tile * 128
        inside = jnp.where((lanes >= first) & (lanes < first + HEAD), 1.0, 0.0).astype(BF16)
        return pl.ds(pl.multiple_of(tile * 128, 128), 256), inside

    acc_v[0] = jnp.zeros((TOK, D), F32)
    loads[1].wait()
    loads[2].wait()
    loads[3].wait()
    scale = 1.0 / math.sqrt(HEAD)

    @pl.loop(0, HEADS // 2)
    def _(pair_of):
        for one in range(2):
            h = pair_of * 2 + one
            cols, inside = head_window(h)
            scores = nt(q_v[:, cols] * inside, k_v[:, cols]) * scale
            top = jnp.max(scores, axis=1, keepdims=True)
            e = jnp.exp(scores - top)
            weights = e * (1.0 / jnp.sum(e, axis=1, keepdims=True))
            attn_v[h] = weights
            acc_v[0, :, cols] += nn(weights.astype(BF16), v_v[:, cols] * inside)

    @pl.loop(0, 5)
    def _(n):
        cols = pl.ds(pl.multiple_of(n * 256, 256), 256)
        mixed_v[:, cols] = acc_v[0, :, cols].astype(BF16)

    loads[4].wait()
    loads[5].wait()

    @pl.loop(0, 5)
    def _(n):
        cols = pl.ds(pl.multiple_of(n * 256, 256), 256)
        stream = res_v[:, cols].astype(F32) + nn(mixed_v[...], proj_v[:, cols])
        acc_v[2, :, cols] = stream.astype(BF16).astype(F32)

    gain_row = gain_ref[...]

    @pl.loop(0, 8)
    def _(b):
        rows = pl.ds(pl.multiple_of(b * 32, 32), 32)
        stream = acc_v[2, rows, :]
        centred = stream - jnp.mean(stream, axis=1, keepdims=True)
        rstd = lax.rsqrt(jnp.mean(centred * centred, axis=1, keepdims=True) + EPS)
        scaled = centred * rstd
        acc_v[2, rows, :] = scaled
        rstd_v[rows, :] = jnp.broadcast_to(rstd, (32, 128))
        enter_v[rows, :] = (scaled * gain_row).astype(BF16)

    @pl.loop(0, 5)
    def _(n):
        rows = nn(pick_v[...], two_lanes(enter_v, n))
        send_b[:, :, pl.ds(pl.multiple_of(n * 128, 128), 128)] = pack(rows)

    own_enter = dispatch(1, send_b, enter_recv)

    pair_mixed = pair(2, mixed_v, mixed_p)
    pair_mixed.start()

    @pl.loop(0, 8)
    def _(b):
        rows = pl.ds(pl.multiple_of(b * 32, 32), 32)
        total = cot_v[0, rows, :].astype(F32)
        for m in range(1, MEMBERS):
            total += cot_v[m, rows, :].astype(F32)
        acc_v[0, rows, :] = total

    def unpack_rows(src, dst, start, count):
        @pl.loop(0, count // 8)
        def _(g):
            chunk = src[pl.ds(start + g * 8, 8)].astype(F32)
            rows = pl.ds(pl.multiple_of(start * 8 + g * 64, 64), 64)
            dst[rows, :HALF] = chunk[:, :CAP, :].reshape(64, HALF).astype(BF16)
            dst[rows, HALF:] = chunk[:, CAP:, :].reshape(64, HALF).astype(BF16)

    own_grad.wait()
    wait_landed(0, grad_recv, 1, 31)
    wait_landed(1, grad_recv, 32, 32)
    unpack_rows(grad_recv, grad_v, 0, CHIPS)
    pair_grad = pair(3, grad_v, grad_p)
    pair_grad.start()
    loads[6].wait()
    pair_second.wait_recv()

    @pl.loop(0, 10)
    def _(t):
        cols = pl.ds(pl.multiple_of(t * 256, 256), 256)
        dpre_v[:, cols] = nt(grad_v[...], second_v[cols, :]).astype(BF16)

    wait_sent(0, send_a, 63)
    loads[7].wait()
    pair_first.wait_recv()

    diagonal = jnp.where(
        lax.broadcasted_iota(jnp.int32, (CAP, 128), 0) == lax.broadcasted_iota(jnp.int32, (CAP, 128), 1), 1.0, 0.0
    )
    pair_enter = []
    for b in range(ROWS // BLOCK):
        chunks = BLOCK // CAP
        if b == 0:
            own_enter.wait()
            wait_landed(2, enter_recv, 1, 31)
        else:
            wait_landed(3, enter_recv, 32, 32)
        unpack_rows(enter_recv, enter_rows, b * chunks, chunks)
        block = pl.ds(b * BLOCK, BLOCK)
        item = pair(4 + b, enter_rows.at[block], enter_p.at[block])
        item.start()
        pair_enter.append(item)
        dot_v[...] = jnp.zeros((BLOCK, 128), F32)

        @pl.loop(0, 10)
        def _(t, block=block):
            cols = pl.ds(pl.multiple_of(t * 256, 256), 256)
            pre = nn(enter_rows[block, :], first_v[:, cols])
            value, slope = gelu_with_grad(pre)
            hidden = value.astype(BF16)
            d_hidden = dpre_v[block, cols].astype(F32)
            hidden_v[block, cols] = hidden
            dpre_v[block, cols] = (slope * d_hidden).astype(BF16)
            both = hidden.astype(F32) * d_hidden
            dot_v[...] += both[:, :128] + both[:, 128:]

        @pl.loop(0, 5)
        def _(n, block=block, b=b, chunks=chunks):
            low = pl.ds(pl.multiple_of(n * 128, 128), 128)
            high = pl.ds(pl.multiple_of(HALF + n * 128, 128), 128)
            weights = jnp.concatenate([first_v[low, :], first_v[high, :]], axis=0)
            send_a[b * chunks : (b + 1) * chunks, :, low] = pack(nt(dpre_v[block, :], weights))

        if b == 0:
            own_back = pltpu.make_async_copy(send_a.at[0], back_recv.at[chip], local_sem.at[2])
            own_back.start()

        @pl.loop(max(1, b * chunks), (b + 1) * chunks)
        def _(n):
            pltpu.make_async_remote_copy(
                send_a.at[n], back_recv.at[chip], a2a_send.at[2], a2a_recv.at[4],
                device_id=(core, behind(n)), device_id_type=MESH,
            ).start()

        dots = jnp.sum(dot_v[...], axis=1, keepdims=True).reshape(chunks, CAP, 1)
        gate_send[b * chunks : (b + 1) * chunks] = jnp.sum(dots * diagonal, axis=1, keepdims=True)

    pair_hidden = pair(6, hidden_v.at[:, pl.ds(D, D)], hidden_p)
    pair_dpre = pair(7, dpre_v.at[:, pl.ds(D, D)], dpre_p)
    pair_hidden.start()
    pair_dpre.start()

    own_gate = pltpu.make_async_copy(gate_send.at[0], gate_recv.at[chip], local_sem.at[3])
    own_gate.start()

    @pl.loop(1, CHIPS)
    def _(n):
        pltpu.make_async_remote_copy(
            gate_send.at[n], gate_recv.at[chip], a2a_send.at[3], a2a_recv.at[5],
            device_id=(core, behind(n)), device_id_type=MESH,
        ).start()

    pair_grad.wait_recv()
    for item in pair_enter:
        item.wait_recv()
    pair_hidden.wait_recv()

    @pl.loop(0, 5)
    def _(t):
        cols = pl.ds(pl.multiple_of(t * 256, 256), 256)
        total = tn(hidden_v[:, cols], grad_v[...]) + tn(hidden_p[:, cols], grad_p[...])
        second_v[cols, :] = total.astype(BF16)

    store_second = pltpu.make_async_copy(second_v.at[pl.ds(0, D)], second_out.at[0], store_sem.at[0])
    store_second.start()
    pair_dpre.wait_recv()

    @pl.loop(0, 5)
    def _(t):
        cols = pl.ds(pl.multiple_of(t * 256, 256), 256)
        total = tn(enter_rows[:, cols], dpre_v[:, :D]) + tn(enter_p[:, cols], dpre_p[...])
        first_v[cols, :D] = total.astype(BF16)

    store_first = pltpu.make_async_copy(first_v.at[:, pl.ds(0, D)], first_out.at[0], store_sem.at[1])
    store_first.start()

    own_back.wait()
    wait_landed(4, back_recv, 0, 63)

    @pl.loop(0, 5)
    def _(n):
        low = pl.ds(pl.multiple_of(n * 128, 128), 128)
        high = pl.ds(pl.multiple_of(HALF + n * 128, 128), 128)
        chunk = back_recv[:, :, low].astype(F32)
        rows = jnp.concatenate(
            [chunk[:, :CAP, :].reshape(ROWS, 128), chunk[:, CAP:, :].reshape(ROWS, 128)], axis=1
        ).astype(BF16)
        total = tn(pick_v[...], rows)
        acc_v[1, :, low] = total[:, :128]
        acc_v[1, :, high] = total[:, 128:]

    @pl.loop(0, 8)
    def _(b):
        rows = pl.ds(pl.multiple_of(b * 32, 32), 32)
        d_norm = acc_v[1, rows, :]
        scaled = acc_v[2, rows, :]
        by_gain = (d_norm * scaled).astype(BF16)
        d_scaled = d_norm * gain_row
        mean_d = jnp.mean(d_scaled, axis=1, keepdims=True)
        mean_ds = jnp.mean(d_scaled * scaled, axis=1, keepdims=True)
        d_stream = rstd_v[rows, :1] * (d_scaled - mean_d - scaled * mean_ds)
        grad = (acc_v[0, rows, :] + d_stream).astype(BF16)
        resid_v[rows, :] = grad
        for half in range(2):
            rg_v[half, rows, :HALF] = grad[:, half * HALF : (half + 1) * HALF]
            rg_v[half, rows, HALF:] = by_gain[:, half * HALF : (half + 1) * HALF]

    pair_rg = pair(8, rg_v.at[1 - core], rg_p)
    pair_rg.start()
    store_resid = pltpu.make_async_copy(resid_v, resid_out, store_sem.at[2])
    store_resid.start()

    @pl.loop(0, 5)
    def _(n):
        cols = pl.ds(pl.multiple_of(n * 256, 256), 256)
        dmix_v[:, cols] = nt(resid_v[...], proj_v[cols, :]).astype(BF16)

    pair_mixed.wait_recv()
    pair_rg.wait_recv()
    loads[8].wait()
    for n, (order, at) in enumerate(((0, 0), (1, 0), (1, HALF))):
        perm_v[n, 0] = nn(rg_v[core, :, at : at + HALF], order_v[order]).astype(BF16)
        perm_v[n, 1] = nn(rg_p[:, at : at + HALF], order_v[order]).astype(BF16)

    @pl.loop(0, 5)
    def _(t):
        cols = pl.ds(pl.multiple_of(t * 128, 128), 128)
        sum1[0, cols, :] = (
            tn(rg_v[core, :, cols], mixed_v[:, :LANES]) + tn(rg_p[:, cols], mixed_p[:, :LANES])
        ).astype(BF16)
        sum1[1, cols, :] = (
            tn(perm_v[0, 0, :, cols], mixed_v[:, LANES : 2 * LANES])
            + tn(perm_v[0, 1, :, cols], mixed_p[:, LANES : 2 * LANES])
        ).astype(BF16)
        sum1[2, cols, :256] = (
            tn(perm_v[1, 0, :, cols], mixed_v[:, 2 * LANES :]) + tn(perm_v[1, 1, :, cols], mixed_p[:, 2 * LANES :])
        ).astype(BF16)
        ones = jnp.ones((TOK, 256), BF16)
        sum1[2, cols, 256:] = (tn(perm_v[2, 0, :, cols], ones) + tn(perm_v[2, 1, :, cols], ones)).astype(BF16)

    axes = ((0, 1, 2), (1, 0, 2), (2, 0, 1))

    def hop(stage, part, o):
        axis = axes[part][stage]
        to = (place[axis] + o) % 4
        spot = [to if a == axis else place[a] for a in range(3)]
        target = spot[0] * 16 + spot[1] * 4 + spot[2]
        if stage == 0:
            src, dst = sum1.at[part, pl.ds(pl.multiple_of(to * 160, 160), 160)], recv1.at[part, o - 1]
        elif stage == 1:
            src, dst = sum2.at[part, to], recv2.at[part, o - 1]
        else:
            src, dst = sum3.at[part, to], recv3.at[part, o - 1]
        n = (stage * 3 + part) * 3 + o - 1
        return pltpu.make_async_remote_copy(
            src, dst, rs_send.at[n], rs_recv.at[n], device_id=(core, target), device_id_type=MESH
        )

    hops = [[hop(s, p, o) for p in range(3) for o in (1, 3, 2)] for s in range(3)]

    def gathered(stage, part):
        mine = place[axes[part][stage]]
        if stage == 0:
            own, others = sum1[part, pl.ds(pl.multiple_of(mine * 160, 160), 160), :], recv1
        elif stage == 1:
            own, others = sum2[part, mine], recv2
        else:
            own, others = sum3[part, mine], recv3
        total = own.astype(F32)
        for o in range(3):
            total += others[part, o].astype(F32)
        return total

    for item in hops[0]:
        item.start()

    acc_v[...] = jnp.zeros((3, TOK, D), F32)

    def attention_back(start, stop):
        @pl.loop(start, stop)
        def _(pair_of):
            for one in range(2):
                h = pair_of * 2 + one
                cols, inside = head_window(h)
                d_mixed = dmix_v[:, cols] * inside
                weights = attn_v[h]
                d_weights = nt(d_mixed, v_v[:, cols])
                shift = jnp.sum(d_weights * weights, axis=1, keepdims=True)
                d_scores = (weights * (d_weights - shift) * scale).astype(BF16)
                acc_v[0, :, cols] += nn(d_scores, k_v[:, cols] * inside)
                acc_v[1, :, cols] += tn(d_scores, q_v[:, cols] * inside)
                acc_v[2, :, cols] += tn(weights.astype(BF16), d_mixed)

    attention_back(0, 5)
    for item in hops[0]:
        item.wait_recv()
    for part in range(3):
        total = gathered(0, part)
        for t in range(4):
            sum2[part, t] = jnp.concatenate([total[t * 40 : (t + 1) * 40], jnp.zeros((8, LANES), F32)], axis=0).astype(BF16)
    for item in hops[1]:
        item.start()

    attention_back(5, 7)
    for item in hops[1]:
        item.wait_recv()
    row = lax.broadcasted_iota(jnp.int32, (16, 48), 0)
    col = lax.broadcasted_iota(jnp.int32, (16, 48), 1)
    for part in range(3):
        total = gathered(1, part).astype(BF16)
        for t in range(4):
            chosen = jnp.where((col == row + SHARE * t) & (row < SHARE), 1.0, 0.0).astype(BF16)
            sum3[part, t] = nn(chosen, total).astype(BF16)
    for item in hops[2]:
        item.start()

    attention_back(7, 8)
    stores = []
    for n, (staged, out) in enumerate(((q_v, q_out), (k_v, k_out), (v_v, v_out))):

        @pl.loop(0, 5)
        def _(t, n=n, staged=staged):
            cols = pl.ds(pl.multiple_of(t * 256, 256), 256)
            staged[:, cols] = acc_v[n, :, cols].astype(BF16)

        item = pltpu.make_async_copy(staged, out, store_sem.at[3 + n])
        item.start()
        stores.append(item)

    own_gate.wait()
    wait_landed(5, gate_recv, 0, 63)
    for m in range(MEMBERS):
        dots = gate_recv[m * 16 : (m + 1) * 16] * diagonal
        dots = jnp.sum(dots, axis=2, keepdims=True).reshape(128, 1)
        total = jnp.sum(pick_v[m * 128 : (m + 1) * 128, :].astype(F32) * dots, axis=0, keepdims=True)
        gate_out[m : m + 1, :] = total / gates_ref[m : m + 1, :]

    for item in hops[2]:
        item.wait_recv()
    for part in range(3):
        share_out[:, part * LANES : (part + 1) * LANES] = gathered(2, part)

    for stage in hops:
        for item in stage:
            item.wait_send()
    wait_sent(1, send_b, 63)
    wait_sent(2, send_a, 63)
    wait_sent(3, gate_send, 63)
    for item in (pair_second, pair_first, pair_mixed, pair_grad, *pair_enter, pair_hidden, pair_dpre, pair_rg):
        item.wait_send()
    for item in (store_second, store_first, store_resid, *stores):
        item.wait()


def shards(queries, keys_in, values_in, resid, out_proj, ln_gain, w_in, w_out, route, slot, gates, cotangent):
    any_spec = pl.BlockSpec(memory_space=pl.ANY)
    vmem_spec = pl.BlockSpec(memory_space=pltpu.VMEM)
    order = jnp.asarray(block_orders(), BF16)
    tokens = jax.ShapeDtypeStruct((TOK, D), BF16)
    square = jax.ShapeDtypeStruct((1, D, D), BF16)
    bf = lambda *shape: pltpu.VMEM(shape, BF16)
    fl = lambda *shape: pltpu.VMEM(shape, F32)
    dma = lambda n: pltpu.SemaphoreType.DMA((n,))
    resid_grad, query_grad, key_grad, value_grad, share, gate_grad, first_grad, second_grad = pl.pallas_call(
        kernel,
        out_shape=(
            tokens, tokens, tokens, tokens,
            jax.ShapeDtypeStruct((16, 3 * LANES), F32),
            jax.ShapeDtypeStruct((MEMBERS, TOK), F32),
            square, square,
        ),
        in_specs=[any_spec] * 5 + [vmem_spec] + [any_spec] * 2 + [vmem_spec] * 3 + [any_spec] * 2,
        out_specs=(any_spec,) * 4 + (vmem_spec,) * 2 + (any_spec,) * 2,
        scratch_shapes=[
            bf(TOK, D), bf(TOK, D), bf(TOK, D), bf(TOK, D), bf(D, D), bf(MEMBERS, TOK, D), bf(2, HALF, HALF),
            bf(D, H), bf(H, D),
            fl(HEADS, TOK, TOK), fl(3, TOK, D), bf(TOK, D), bf(TOK, D), fl(TOK, 128), bf(TOK, D), bf(ROWS, TOK),
            bf(CHIPS, 16, HALF), bf(CHIPS, 16, HALF), bf(CHIPS, 16, HALF), bf(CHIPS, 16, HALF), bf(CHIPS, 16, HALF),
            bf(ROWS, D), bf(ROWS, D), bf(ROWS, D), bf(ROWS, D), bf(ROWS, H), bf(ROWS, H), bf(ROWS, D), bf(ROWS, D),
            fl(BLOCK, 128),
            bf(2, TOK, D), bf(TOK, D), bf(3, 2, TOK, HALF), bf(TOK, D), bf(TOK, D),
            fl(CHIPS, 1, 128), fl(CHIPS, 1, 128),
            bf(3, HALF, LANES), bf(3, 3, 160, LANES), bf(3, 4, 48, LANES), bf(3, 3, 48, LANES),
            bf(3, 4, 16, LANES), bf(3, 3, 16, LANES),
            dma(9), dma(6), dma(4), dma(9), dma(9), dma(4), dma(6), dma(27), dma(27),
        ],
        compiler_params=pltpu.CompilerParams(
            collective_id=0, has_side_effects=True, vmem_limit_bytes=63 * 1024 * 1024
        ),
        cost_estimate=pl.CostEstimate(flops=25_000_000_000, bytes_accessed=40_000_000, transcendentals=4_000_000),
    )(queries, keys_in, values_in, resid, out_proj, ln_gain[None], w_in, w_out, route, slot, gates, cotangent, order)
    proj_grad = share[:SHARE, :D].T
    gain_grad = share[:SHARE, D]
    return (
        resid_grad, query_grad, key_grad, value_grad, proj_grad, gain_grad, gate_grad, first_grad, second_grad,
    )


def solution(mesh):
    both = ("dp", "expert")
    return jax.shard_map(
        shards,
        mesh=mesh,
        in_specs=(
            P(both, None), P(both, None), P(both, None), P(both, None), P(), P(),
            P("expert", None, "dp"), P("expert", "dp", None),
            P(None, both), P(None, both), P(None, both), P(None, both, None),
        ),
        out_specs=(
            P(both, None), P(both, None), P(both, None), P(both, None), P(None, both), P(both), P(None, both),
            P("expert", None, "dp"), P("expert", "dp", None),
        ),
        check_vma=False,
    )
```

```python
import functools
import math

import jax
import jax.numpy as jnp
import numpy as np
from jax import lax
from jax.experimental import pallas as pl
from jax.experimental.pallas import tpu as pltpu
from jax.sharding import PartitionSpec as P

D = 1280
HALF = 640
HEADS = 16
HEAD = 80
TOK = 256
MEMBERS = 4
CAP = 8
CHIPS = 64
ROWS = CHIPS * CAP
BLOCK = 256
H = 2560
LANES = 512
SHARE = 10
EPS = 1e-06
MESH = pl.DeviceIdType.MESH
F32 = jnp.float32
BF16 = jnp.bfloat16


def product(a, b, contract):
    return lax.dot_general(a, b, (((contract[0],), (contract[1],)), ((), ())), preferred_element_type=F32)


def nn(a, b):
    return product(a, b, (1, 0))


def nt(a, b):
    return product(a, b, (1, 1))


def tn(a, b):
    return product(a, b, (0, 0))


def two_lanes(ref, n, *lead):
    low = pl.multiple_of(n * 128, 128)
    high = pl.multiple_of(HALF + n * 128, 128)
    return jnp.concatenate([ref[(*lead, slice(None), pl.ds(low, 128))], ref[(*lead, slice(None), pl.ds(high, 128))]], axis=1)


def pack(rows):
    count = rows.shape[0] // CAP
    low = rows[:, :128].reshape(count, CAP, 128)
    high = rows[:, 128:].reshape(count, CAP, 128)
    return jnp.concatenate([low, high], axis=1).astype(BF16)


def gelu_with_grad(x):
    below = 1.0 + (0.3275911 * math.sqrt(0.5)) * jnp.abs(x)
    u = pl.reciprocal(below, approx=True)
    u = u * (2.0 - below * u)
    e = jnp.exp(x * x * -0.5)
    poly = u * (0.127414796 + u * (-0.142248368 + u * (0.7107068705 + u * (-0.7265760135 + u * 0.5307027145))))
    tail = poly * e
    cdf = jnp.where(x >= 0.0, 1.0 - tail, tail)
    return x * cdf, cdf + x * (e * (1.0 / math.sqrt(2.0 * math.pi)))


def block_orders():
    d = np.arange(HALF)
    y, x, z, r = d // 160, (d // 40) % 4, (d // 10) % 4, d % 10
    out = np.zeros((2, HALF, HALF), np.float32)
    out[0, d, x * 160 + y * 40 + z * 10 + r] = 1.0
    out[1, d, z * 160 + y * 40 + x * 10 + r] = 1.0
    return out


def kernel(
    q_in, k_in, v_in, res_in, proj_in, gain_ref, first_in, second_in, route_ref, slot_ref, gates_ref, cot_in, order_in,
    resid_out, q_out, k_out, v_out, share_out, gate_out, first_out, second_out,
    q_v, k_v, v_v, res_v, proj_v, cot_v, order_v, first_v, second_v,
    attn_v, acc_v, mixed_v, mixed_p, rstd_v, enter_v, pick_v,
    send_a, send_b, grad_recv, enter_recv, back_recv,
    grad_v, enter_rows, grad_p, enter_p, hidden_v, dpre_v, hidden_p, dpre_p, dot_v,
    rg_v, rg_p, perm_v, resid_v, dmix_v, gate_send, gate_recv,
    sum1, recv1, sum2, recv2, sum3, recv3,
    load_sem, store_sem, local_sem, pair_send, pair_recv, a2a_send, a2a_recv, rs_send, rs_recv,
):
    core = lax.axis_index("dp")
    chip = lax.axis_index("expert")
    place = (chip // 16, (chip // 4) % 4, chip % 4)

    around = [[p] + [lax.rem(p + o, 4) for o in range(1, 4)] for p in place]

    def ahead(n):
        o = ((0, 2, 1, 3)[n // 16], (n // 4) % 4, n % 4)
        return around[0][o[0]] * 16 + around[1][o[1]] * 4 + around[2][o[2]]

    def behind(n):
        o = ((0, 2, 3, 1)[n // 16], -(n // 4) % 4, -n % 4)
        return around[0][o[0]] * 16 + around[1][o[1]] * 4 + around[2][o[2]]

    def load(n, src, dst):
        return pltpu.make_async_copy(src, dst, load_sem.at[n])

    loads = [
        load(0, cot_in, cot_v),
        load(1, q_in, q_v),
        load(2, k_in, k_v),
        load(3, v_in, v_v),
        load(4, proj_in, proj_v),
        load(5, res_in, res_v),
        load(6, second_in.at[0], second_v.at[pl.ds(0, D)]),
        load(7, first_in.at[0], first_v.at[:, pl.ds(0, D)]),
        load(8, order_in, order_v),
    ]
    for item in loads:
        item.start()

    barrier = pltpu.get_barrier_semaphore()

    for n in range(1, CHIPS):
        pl.semaphore_signal(barrier, inc=1, device_id=(core, ahead(n)), device_id_type=MESH)

    pl.semaphore_signal(barrier, inc=1, device_id=(1 - core, chip), device_id_type=MESH)

    def pair(n, src, dst):
        return pltpu.make_async_remote_copy(
            src, dst, pair_send.at[n], pair_recv.at[n], device_id=(1 - core, chip), device_id_type=MESH
        )

    row_iota = lax.broadcasted_iota(jnp.int32, (MEMBERS * 32, TOK), 0)
    row_of = jnp.where(slot_ref[...] < CAP, route_ref[...] * CAP + slot_ref[...], -1)
    loads[0].wait()
    for m in range(MEMBERS):
        picked = jnp.where(row_iota == row_of[m : m + 1, :], 1.0, 0.0)
        pick_v[m * 128 : (m + 1) * 128, :] = picked.astype(BF16)
        gate_rows = jnp.sum(picked * gates_ref[m : m + 1, :], axis=1, keepdims=True)

        @pl.loop(0, 5)
        def _(n, m=m, gate_rows=gate_rows):
            rows = nn(pick_v[m * 128 : (m + 1) * 128, :], two_lanes(cot_v, n, m)) * gate_rows
            send_a[m * 16 : (m + 1) * 16, :, pl.ds(pl.multiple_of(n * 128, 128), 128)] = pack(rows)

    pl.semaphore_wait(barrier, CHIPS)

    pair_second = pair(0, second_in.at[0], second_v.at[pl.ds(D, D)])
    pair_first = pair(1, first_in.at[0], first_v.at[:, pl.ds(D, D)])
    pair_second.start()
    pair_first.start()

    def dispatch(which, src, dst):
        own = pltpu.make_async_copy(src.at[chip], dst.at[0], local_sem.at[which])
        own.start()

        for n in range(1, CHIPS):
            to = ahead(n)
            pltpu.make_async_remote_copy(
                src.at[to], dst.at[n], a2a_send.at[which], a2a_recv.at[which * 2 + n // 32],
                device_id=(core, to), device_id_type=MESH,
            ).start()

        return own

    def wait_sent(which, ref, count):
        pltpu.make_async_remote_copy(
            ref.at[pl.ds(0, count)], ref.at[pl.ds(0, count)], a2a_send.at[which], a2a_recv.at[which * 2],
            device_id=(1 - core, chip), device_id_type=MESH,
        ).wait_send()

    def wait_landed(n, ref, start, count):
        pltpu.make_async_remote_copy(
            ref.at[pl.ds(start, count)], ref.at[pl.ds(start, count)], a2a_send.at[0], a2a_recv.at[n],
            device_id=(1 - core, chip), device_id_type=MESH,
        ).wait_recv()

    own_grad = dispatch(0, send_a, grad_recv)

    def head_window(h):
        tile = (h * HEAD) // 128
        tile = tile - tile // 9
        lanes = lax.broadcasted_iota(jnp.int32, (1, 256), 1)
        first = h * HEAD - tile * 128
        inside = jnp.where((lanes >= first) & (lanes < first + HEAD), 1.0, 0.0).astype(BF16)
        return pl.ds(pl.multiple_of(tile * 128, 128), 256), inside

    acc_v[0] = jnp.zeros((TOK, D), F32)
    loads[1].wait()
    loads[2].wait()
    loads[3].wait()
    scale = 1.0 / math.sqrt(HEAD)

    @pl.loop(0, HEADS // 4)
    def _(four):
        for one in range(4):
            h = four * 4 + one
            cols, inside = head_window(h)
            scores = nt(q_v[:, cols] * inside, k_v[:, cols]) * scale
            top = jnp.max(scores, axis=1, keepdims=True)
            e = jnp.exp(scores - top)
            weights = e * (1.0 / jnp.sum(e, axis=1, keepdims=True))
            attn_v[h] = weights
            acc_v[0, :, cols] += nn(weights.astype(BF16), v_v[:, cols] * inside)

    @pl.loop(0, 5)
    def _(n):
        cols = pl.ds(pl.multiple_of(n * 256, 256), 256)
        mixed_v[:, cols] = acc_v[0, :, cols].astype(BF16)

    loads[4].wait()
    loads[5].wait()

    @pl.loop(0, 5)
    def _(n):
        cols = pl.ds(pl.multiple_of(n * 256, 256), 256)
        stream = res_v[:, cols].astype(F32) + nn(mixed_v[...], proj_v[:, cols])
        acc_v[2, :, cols] = stream.astype(BF16).astype(F32)

    gain_row = gain_ref[...].reshape(1, D)

    @pl.loop(0, 8)
    def _(b):
        rows = pl.ds(pl.multiple_of(b * 32, 32), 32)
        stream = acc_v[2, rows, :]
        centred = stream - jnp.mean(stream, axis=1, keepdims=True)
        rstd = lax.rsqrt(jnp.mean(centred * centred, axis=1, keepdims=True) + EPS)
        scaled = centred * rstd
        acc_v[2, rows, :] = scaled
        rstd_v[rows, :] = jnp.broadcast_to(rstd, (32, 128))
        enter_v[rows, :] = (scaled * gain_row).astype(BF16)

    @pl.loop(0, 5)
    def _(n):
        rows = nn(pick_v[...], two_lanes(enter_v, n))
        send_b[:, :, pl.ds(pl.multiple_of(n * 128, 128), 128)] = pack(rows)

    own_enter = dispatch(1, send_b, enter_recv)

    pair_mixed = pair(2, mixed_v, mixed_p)
    pair_mixed.start()

    @pl.loop(0, 8)
    def _(b):
        rows = pl.ds(pl.multiple_of(b * 32, 32), 32)
        total = cot_v[0, rows, :].astype(F32)
        for m in range(1, MEMBERS):
            total += cot_v[m, rows, :].astype(F32)
        acc_v[0, rows, :] = total

    def unpack_rows(src, dst, start, count):
        @pl.loop(0, count // 8)
        def _(g):
            chunk = src[pl.ds(start + g * 8, 8)].astype(F32)
            rows = pl.ds(pl.multiple_of(start * 8 + g * 64, 64), 64)
            dst[rows, :HALF] = chunk[:, :CAP, :].reshape(64, HALF).astype(BF16)
            dst[rows, HALF:] = chunk[:, CAP:, :].reshape(64, HALF).astype(BF16)

    own_grad.wait()
    wait_landed(0, grad_recv, 1, 31)
    wait_landed(1, grad_recv, 32, 32)
    unpack_rows(grad_recv, grad_v, 0, CHIPS)
    pair_grad = pair(3, grad_v, grad_p)
    pair_grad.start()
    loads[6].wait()
    pair_second.wait_recv()

    @pl.loop(0, 10)
    def _(t):
        cols = pl.ds(pl.multiple_of(t * 256, 256), 256)
        dpre_v[:, cols] = nt(grad_v[...], second_v[cols, :]).astype(BF16)

    wait_sent(0, send_a, 63)
    loads[7].wait()
    pair_first.wait_recv()

    diagonal = jnp.where(
        lax.broadcasted_iota(jnp.int32, (CAP, 128), 0) == lax.broadcasted_iota(jnp.int32, (CAP, 128), 1), 1.0, 0.0
    )
    pair_enter = []
    for b in range(ROWS // BLOCK):
        chunks = BLOCK // CAP
        if b == 0:
            own_enter.wait()
            wait_landed(2, enter_recv, 1, 31)
        else:
            wait_landed(3, enter_recv, 32, 32)
        unpack_rows(enter_recv, enter_rows, b * chunks, chunks)
        block = pl.ds(b * BLOCK, BLOCK)
        item = pair(4 + b, enter_rows.at[block], enter_p.at[block])
        item.start()
        pair_enter.append(item)
        dot_v[...] = jnp.zeros((BLOCK, 128), F32)

        dot_v[...] = jnp.zeros((BLOCK, 128), F32)

        @pl.loop(0, 10, unroll=2)
        def _(t, block=block):
            cols = pl.ds(pl.multiple_of(t * 256, 256), 256)
            pre = nn(enter_rows[block, :], first_v[:, cols])
            value, slope = gelu_with_grad(pre)
            hidden = value.astype(BF16)
            d_hidden = dpre_v[block, cols].astype(F32)
            hidden_v[block, cols] = hidden
            dpre_v[block, cols] = (slope * d_hidden).astype(BF16)
            both = value * d_hidden
            dot_v[...] += both[:, :128] + both[:, 128:]

        @pl.loop(0, 5)
        def _(n, block=block, b=b, chunks=chunks):
            low = pl.ds(pl.multiple_of(n * 128, 128), 128)
            high = pl.ds(pl.multiple_of(HALF + n * 128, 128), 128)
            weights = jnp.concatenate([first_v[low, :], first_v[high, :]], axis=0)
            send_a[b * chunks : (b + 1) * chunks, :, low] = pack(nt(dpre_v[block, :], weights))

        if b == 0:
            own_back = pltpu.make_async_copy(send_a.at[0], back_recv.at[chip], local_sem.at[2])
            own_back.start()

        for n in range(max(1, b * chunks), (b + 1) * chunks):
            pltpu.make_async_remote_copy(
                send_a.at[n], back_recv.at[chip], a2a_send.at[2], a2a_recv.at[4],
                device_id=(core, behind(n)), device_id_type=MESH,
            ).start()

        dots = jnp.sum(dot_v[...], axis=1, keepdims=True).reshape(chunks, CAP, 1)
        gate_send[b * chunks : (b + 1) * chunks] = jnp.sum(dots * diagonal, axis=1, keepdims=True)

    pair_hidden = pair(6, hidden_v.at[:, pl.ds(D, D)], hidden_p)
    pair_dpre = pair(7, dpre_v.at[:, pl.ds(D, D)], dpre_p)
    pair_hidden.start()
    pair_dpre.start()

    own_gate = pltpu.make_async_copy(gate_send.at[0], gate_recv.at[chip], local_sem.at[3])
    own_gate.start()

    for n in range(1, CHIPS):
        pltpu.make_async_remote_copy(
            gate_send.at[n], gate_recv.at[chip], a2a_send.at[3], a2a_recv.at[5],
            device_id=(core, behind(n)), device_id_type=MESH,
        ).start()

    pair_grad.wait_recv()
    for item in pair_enter:
        item.wait_recv()
    pair_hidden.wait_recv()

    @pl.loop(0, 5)
    def _(t):
        cols = pl.ds(pl.multiple_of(t * 256, 256), 256)
        total = tn(hidden_v[:, cols], grad_v[...]) + tn(hidden_p[:, cols], grad_p[...])
        second_v[cols, :] = total.astype(BF16)

    store_second = pltpu.make_async_copy(second_v.at[pl.ds(0, D)], second_out.at[0], store_sem.at[0])
    store_second.start()
    pair_dpre.wait_recv()

    @pl.loop(0, 5)
    def _(t):
        cols = pl.ds(pl.multiple_of(t * 256, 256), 256)
        total = tn(enter_rows[:, cols], dpre_v[:, :D]) + tn(enter_p[:, cols], dpre_p[...])
        first_v[cols, :D] = total.astype(BF16)

    store_first = pltpu.make_async_copy(first_v.at[:, pl.ds(0, D)], first_out.at[0], store_sem.at[1])
    store_first.start()

    own_back.wait()
    wait_landed(4, back_recv, 0, 63)

    @pl.loop(0, 5)
    def _(n):
        low = pl.ds(pl.multiple_of(n * 128, 128), 128)
        high = pl.ds(pl.multiple_of(HALF + n * 128, 128), 128)
        chunk = back_recv[:, :, low].astype(F32)
        rows = jnp.concatenate(
            [chunk[:, :CAP, :].reshape(ROWS, 128), chunk[:, CAP:, :].reshape(ROWS, 128)], axis=1
        ).astype(BF16)
        total = tn(pick_v[...], rows)
        acc_v[1, :, low] = total[:, :128]
        acc_v[1, :, high] = total[:, 128:]

    @pl.loop(0, 8)
    def _(b):
        rows = pl.ds(pl.multiple_of(b * 32, 32), 32)
        d_norm = acc_v[1, rows, :]
        scaled = acc_v[2, rows, :]
        by_gain = (d_norm * scaled).astype(BF16)
        d_scaled = d_norm * gain_row
        mean_d = jnp.mean(d_scaled, axis=1, keepdims=True)
        mean_ds = jnp.mean(d_scaled * scaled, axis=1, keepdims=True)
        d_stream = rstd_v[rows, :1] * (d_scaled - mean_d - scaled * mean_ds)
        grad = (acc_v[0, rows, :] + d_stream).astype(BF16)
        resid_v[rows, :] = grad
        for half in range(2):
            rg_v[half, rows, :HALF] = grad[:, half * HALF : (half + 1) * HALF]
            rg_v[half, rows, HALF:] = by_gain[:, half * HALF : (half + 1) * HALF]

    pair_rg = pair(8, rg_v.at[1 - core], rg_p)
    pair_rg.start()
    store_resid = pltpu.make_async_copy(resid_v, resid_out, store_sem.at[2])
    store_resid.start()

    @pl.loop(0, 5)
    def _(n):
        cols = pl.ds(pl.multiple_of(n * 256, 256), 256)
        dmix_v[:, cols] = nt(resid_v[...], proj_v[cols, :]).astype(BF16)

    pair_mixed.wait_recv()
    pair_rg.wait_recv()
    loads[8].wait()
    for n, (order, at) in enumerate(((0, 0), (1, 0), (1, HALF))):
        perm_v[n, 0] = nn(rg_v[core, :, at : at + HALF], order_v[order]).astype(BF16)
        perm_v[n, 1] = nn(rg_p[:, at : at + HALF], order_v[order]).astype(BF16)

    @pl.loop(0, 5)
    def _(t):
        cols = pl.ds(pl.multiple_of(t * 128, 128), 128)
        sum1[0, cols, :] = (
            tn(rg_v[core, :, cols], mixed_v[:, :LANES]) + tn(rg_p[:, cols], mixed_p[:, :LANES])
        ).astype(BF16)
        sum1[1, cols, :] = (
            tn(perm_v[0, 0, :, cols], mixed_v[:, LANES : 2 * LANES])
            + tn(perm_v[0, 1, :, cols], mixed_p[:, LANES : 2 * LANES])
        ).astype(BF16)
        sum1[2, cols, :256] = (
            tn(perm_v[1, 0, :, cols], mixed_v[:, 2 * LANES :]) + tn(perm_v[1, 1, :, cols], mixed_p[:, 2 * LANES :])
        ).astype(BF16)
        ones = jnp.ones((TOK, 256), BF16)
        sum1[2, cols, 256:] = (tn(perm_v[2, 0, :, cols], ones) + tn(perm_v[2, 1, :, cols], ones)).astype(BF16)

    axes = ((0, 1, 2), (1, 0, 2), (2, 0, 1))

    def hop(stage, part, o):
        axis = axes[part][stage]
        to = (place[axis] + o) % 4
        spot = [to if a == axis else place[a] for a in range(3)]
        target = spot[0] * 16 + spot[1] * 4 + spot[2]
        if stage == 0:
            src, dst = sum1.at[part, pl.ds(pl.multiple_of(to * 160, 160), 160)], recv1.at[part, o - 1]
        elif stage == 1:
            src, dst = sum2.at[part, to], recv2.at[part, o - 1]
        else:
            src, dst = sum3.at[part, to], recv3.at[part, o - 1]
        n = (stage * 3 + part) * 3 + o - 1
        return pltpu.make_async_remote_copy(
            src, dst, rs_send.at[n], rs_recv.at[n], device_id=(core, target), device_id_type=MESH
        )

    hops = [[hop(s, p, o) for p in range(3) for o in (1, 3, 2)] for s in range(3)]

    def gathered(stage, part):
        mine = place[axes[part][stage]]
        if stage == 0:
            own, others = sum1[part, pl.ds(pl.multiple_of(mine * 160, 160), 160), :], recv1
        elif stage == 1:
            own, others = sum2[part, mine], recv2
        else:
            own, others = sum3[part, mine], recv3
        total = own.astype(F32)
        for o in range(3):
            total += others[part, o].astype(F32)
        return total

    for item in hops[0]:
        item.start()

    acc_v[...] = jnp.zeros((3, TOK, D), F32)

    def attention_back(start, stop):
        @pl.loop(start, stop)
        def _(four):
            for one in range(4):
                h = four * 4 + one
                cols, inside = head_window(h)
                d_mixed = dmix_v[:, cols] * inside
                weights = attn_v[h]
                d_weights = nt(d_mixed, v_v[:, cols])
                shift = jnp.sum(d_weights * weights, axis=1, keepdims=True)
                d_scores = (weights * (d_weights - shift) * scale).astype(BF16)
                acc_v[0, :, cols] += nn(d_scores, k_v[:, cols] * inside)
                acc_v[1, :, cols] += tn(d_scores, q_v[:, cols] * inside)
                acc_v[2, :, cols] += tn(weights.astype(BF16), d_mixed)

    attention_back(0, 2)
    for item in hops[0]:
        item.wait_recv()
    for part in range(3):
        total = gathered(0, part)
        for t in range(4):
            sum2[part, t] = jnp.concatenate([total[t * 40 : (t + 1) * 40], jnp.zeros((8, LANES), F32)], axis=0).astype(BF16)
    for item in hops[1]:
        item.start()

    attention_back(2, 3)
    for item in hops[1]:
        item.wait_recv()
    row = lax.broadcasted_iota(jnp.int32, (16, 48), 0)
    col = lax.broadcasted_iota(jnp.int32, (16, 48), 1)
    for part in range(3):
        total = gathered(1, part).astype(BF16)
        for t in range(4):
            chosen = jnp.where((col == row + SHARE * t) & (row < SHARE), 1.0, 0.0).astype(BF16)
            sum3[part, t] = nn(chosen, total).astype(BF16)
    for item in hops[2]:
        item.start()

    attention_back(3, 4)
    stores = []
    for n, (staged, out) in enumerate(((q_v, q_out), (k_v, k_out), (v_v, v_out))):

        @pl.loop(0, 5)
        def _(t, n=n, staged=staged):
            cols = pl.ds(pl.multiple_of(t * 256, 256), 256)
            staged[:, cols] = acc_v[n, :, cols].astype(BF16)

        item = pltpu.make_async_copy(staged, out, store_sem.at[3 + n])
        item.start()
        stores.append(item)

    own_gate.wait()
    wait_landed(5, gate_recv, 0, 63)
    for m in range(MEMBERS):
        dots = gate_recv[m * 16 : (m + 1) * 16] * diagonal
        dots = jnp.sum(dots, axis=2, keepdims=True).reshape(128, 1)
        total = jnp.sum(pick_v[m * 128 : (m + 1) * 128, :].astype(F32) * dots, axis=0, keepdims=True)
        gate_out[m : m + 1, :] = total / gates_ref[m : m + 1, :]

    for item in hops[2]:
        item.wait_recv()
    for part in range(3):
        share_out[:, part * LANES : (part + 1) * LANES] = gathered(2, part)

    for stage in hops:
        for item in stage:
            item.wait_send()
    wait_sent(1, send_b, 63)
    wait_sent(2, send_a, 63)
    wait_sent(3, gate_send, 63)
    for item in (pair_second, pair_first, pair_mixed, pair_grad, *pair_enter, pair_hidden, pair_dpre, pair_rg):
        item.wait_send()
    for item in (store_second, store_first, store_resid, *stores):
        item.wait()


def finish(
    resid_in, q_in, k_in, v_in, first_in, second_in, share_ref, gate_ref,
    resid_out, q_out, k_out, v_out, first_out, second_out, proj_out, gain_out, gate_out,
    wide_v, rows_v, sem,
):
    pieces = [
        (first_in.at[0, pl.ds(0, HALF)], first_out.at[0, pl.ds(0, HALF)], wide_v.at[0, 0]),
        (second_in.at[0, pl.ds(0, HALF)], second_out.at[0, pl.ds(0, HALF)], wide_v.at[1, 0]),
        (first_in.at[0, pl.ds(HALF, HALF)], first_out.at[0, pl.ds(HALF, HALF)], wide_v.at[0, 1]),
        (second_in.at[0, pl.ds(HALF, HALF)], second_out.at[0, pl.ds(HALF, HALF)], wide_v.at[1, 1]),
        (resid_in, resid_out, rows_v.at[0]),
        (q_in, q_out, rows_v.at[1]),
        (k_in, k_out, rows_v.at[2]),
        (v_in, v_out, rows_v.at[3]),
    ]
    loads = [pltpu.make_async_copy(src, held, sem.at[0, n]) for n, (src, _, held) in enumerate(pieces)]
    stores = [pltpu.make_async_copy(held, dst, sem.at[1, n]) for n, (_, dst, held) in enumerate(pieces)]
    for item in loads:
        item.start()
    for load, store in zip(loads, stores):
        load.wait()
        store.start()
    proj_out[...] = share_ref[:SHARE, :D]
    row = lax.broadcasted_iota(jnp.int32, (16, 128), 0)
    col = lax.broadcasted_iota(jnp.int32, (16, 128), 1)
    gain = jnp.sum(jnp.where(row == col, share_ref[:, D : D + 128], 0.0), axis=0, keepdims=True)
    gain_out[...] = gain[:, :SHARE]
    gate_out[...] = gate_ref[...]
    for item in stores:
        item.wait()


def shards(queries, keys_in, values_in, resid, out_proj, ln_gain, w_in, w_out, route, slot, gates, cotangent):
    any_spec = pl.BlockSpec(memory_space=pl.ANY)
    vmem_spec = pl.BlockSpec(memory_space=pltpu.VMEM)
    order = jnp.asarray(block_orders(), BF16)
    tokens = jax.ShapeDtypeStruct((TOK, D), BF16)
    square = jax.ShapeDtypeStruct((1, D, D), BF16)
    bf = lambda *shape: pltpu.VMEM(shape, BF16)
    fl = lambda *shape: pltpu.VMEM(shape, F32)
    dma = lambda n: pltpu.SemaphoreType.DMA((n,))
    resid_grad, query_grad, key_grad, value_grad, share, gate_grad, first_grad, second_grad = pl.pallas_call(
        kernel,
        out_shape=(
            tokens, tokens, tokens, tokens,
            jax.ShapeDtypeStruct((16, 3 * LANES), F32),
            jax.ShapeDtypeStruct((MEMBERS, TOK), F32),
            square, square,
        ),
        in_specs=[any_spec] * 5 + [vmem_spec] + [any_spec] * 2 + [vmem_spec] * 3 + [any_spec] * 2,
        out_specs=(any_spec,) * 4 + (vmem_spec,) * 2 + (any_spec,) * 2,
        scratch_shapes=[
            bf(TOK, D), bf(TOK, D), bf(TOK, D), bf(TOK, D), bf(D, D), bf(MEMBERS, TOK, D), bf(2, HALF, HALF),
            bf(D, H), bf(H, D),
            fl(HEADS, TOK, TOK), fl(3, TOK, D), bf(TOK, D), bf(TOK, D), fl(TOK, 128), bf(TOK, D), bf(ROWS, TOK),
            bf(CHIPS, 16, HALF), bf(CHIPS, 16, HALF), bf(CHIPS, 16, HALF), bf(CHIPS, 16, HALF), bf(CHIPS, 16, HALF),
            bf(ROWS, D), bf(ROWS, D), bf(ROWS, D), bf(ROWS, D), bf(ROWS, H), bf(ROWS, H), bf(ROWS, D), bf(ROWS, D),
            fl(BLOCK, 128),
            bf(2, TOK, D), bf(TOK, D), bf(3, 2, TOK, HALF), bf(TOK, D), bf(TOK, D),
            fl(CHIPS, 1, 128), fl(CHIPS, 1, 128),
            bf(3, HALF, LANES), bf(3, 3, 160, LANES), bf(3, 4, 48, LANES), bf(3, 3, 48, LANES),
            bf(3, 4, 16, LANES), bf(3, 3, 16, LANES),
            dma(9), dma(6), dma(4), dma(9), dma(9), dma(4), dma(6), dma(27), dma(27),
        ],
        compiler_params=pltpu.CompilerParams(
            collective_id=0, has_side_effects=True, vmem_limit_bytes=63 * 1024 * 1024
        ),
        cost_estimate=pl.CostEstimate(flops=25_000_000_000, bytes_accessed=40_000_000, transcendentals=4_000_000),
    )(queries, keys_in, values_in, resid, out_proj, ln_gain, w_in, w_out, route, slot, gates, cotangent, order)
    resid_grad, query_grad, key_grad, value_grad, first_grad, second_grad, proj_grad, gain_grad, gate_grad = pl.pallas_call(
        finish,
        out_shape=(
            tokens, tokens, tokens, tokens, square, square,
            jax.ShapeDtypeStruct((SHARE, D), F32),
            jax.ShapeDtypeStruct((1, SHARE), F32),
            jax.ShapeDtypeStruct((MEMBERS, TOK), F32),
        ),
        in_specs=[any_spec] * 6 + [vmem_spec] * 2,
        out_specs=(any_spec,) * 6 + (vmem_spec,) * 3,
        scratch_shapes=[bf(2, 2, HALF, D), bf(4, TOK, D), pltpu.SemaphoreType.DMA((2, 8))],
        compiler_params=pltpu.CompilerParams(vmem_limit_bytes=60 * 1024 * 1024),
    )(resid_grad, query_grad, key_grad, value_grad, first_grad, second_grad, share, gate_grad)
    return (
        resid_grad, query_grad, key_grad, value_grad, proj_grad.T, gain_grad.reshape(SHARE), gate_grad,
        first_grad, second_grad,
    )


def solution(mesh):
    both = ("dp", "expert")
    return jax.shard_map(
        shards,
        mesh=mesh,
        in_specs=(
            P(both, None), P(both, None), P(both, None), P(both, None), P(), P(),
            P("expert", None, "dp"), P("expert", "dp", None),
            P(None, both), P(None, both), P(None, both), P(None, both, None),
        ),
        out_specs=(
            P(both, None), P(both, None), P(both, None), P(both, None), P(None, both), P(both), P(None, both),
            P("expert", None, "dp"), P("expert", "dp", None),
        ),
        check_vma=False,
    )
```

```python
import functools
import math

import jax
import jax.numpy as jnp
import numpy as np
from jax import lax
from jax.experimental import pallas as pl
from jax.experimental.pallas import tpu as pltpu
from jax.sharding import PartitionSpec as P

D = 1280
HALF = 640
HEADS = 16
HEAD = 80
TOK = 256
MEMBERS = 4
CAP = 8
CHIPS = 64
ROWS = CHIPS * CAP
BLOCK = 256
H = 2560
LANES = 512
SHARE = 10
EPS = 1e-06
MESH = pl.DeviceIdType.MESH
F32 = jnp.float32
BF16 = jnp.bfloat16


def product(a, b, contract):
    return lax.dot_general(a, b, (((contract[0],), (contract[1],)), ((), ())), preferred_element_type=F32)


def nn(a, b):
    return product(a, b, (1, 0))


def nt(a, b):
    return product(a, b, (1, 1))


def tn(a, b):
    return product(a, b, (0, 0))


def two_lanes(ref, n, *lead):
    low = pl.multiple_of(n * 128, 128)
    high = pl.multiple_of(HALF + n * 128, 128)
    return jnp.concatenate([ref[(*lead, slice(None), pl.ds(low, 128))], ref[(*lead, slice(None), pl.ds(high, 128))]], axis=1)


def pack(rows):
    count = rows.shape[0] // CAP
    low = rows[:, :128].reshape(count, CAP, 128)
    high = rows[:, 128:].reshape(count, CAP, 128)
    return jnp.concatenate([low, high], axis=1).astype(BF16)


def gelu_with_grad(x):
    below = 1.0 + (0.3275911 * math.sqrt(0.5)) * jnp.abs(x)
    u = pl.reciprocal(below, approx=True)
    u = u * (2.0 - below * u)
    e = jnp.exp(x * x * -0.5)
    poly = u * (0.127414796 + u * (-0.142248368 + u * (0.7107068705 + u * (-0.7265760135 + u * 0.5307027145))))
    tail = poly * e
    cdf = jnp.where(x >= 0.0, 1.0 - tail, tail)
    return x * cdf, cdf + x * (e * (1.0 / math.sqrt(2.0 * math.pi)))


def block_orders():
    d = np.arange(HALF)
    y, x, z, r = d // 160, (d // 40) % 4, (d // 10) % 4, d % 10
    out = np.zeros((2, HALF, HALF), np.float32)
    out[0, d, x * 160 + y * 40 + z * 10 + r] = 1.0
    out[1, d, z * 160 + y * 40 + x * 10 + r] = 1.0
    return out


def kernel(
    q_in, k_in, v_in, res_in, proj_in, gain_ref, first_in, second_in, route_ref, slot_ref, gates_ref, cot_in, order_in,
    resid_out, q_out, k_out, v_out, share_out, gate_out, first_out, second_out,
    q_v, k_v, v_v, res_v, proj_v, cot_v, order_v, first_v, second_v,
    attn_v, acc_v, mixed_v, mixed_p, rstd_v, enter_v, pick_v,
    send_a, send_b, grad_recv, enter_recv, back_recv,
    grad_v, enter_rows, grad_p, enter_p, hidden_v, dpre_v, hidden_p, dpre_p, dot_v,
    rg_v, rg_p, perm_v, resid_v, dmix_v, gate_send, gate_recv,
    sum1, recv1, sum2, recv2, sum3, recv3,
    load_sem, store_sem, local_sem, pair_send, pair_recv, a2a_send, a2a_recv, rs_send, rs_recv,
):
    core = lax.axis_index("dp")
    chip = lax.axis_index("expert")
    place = (chip // 16, (chip // 4) % 4, chip % 4)

    around = [[p] + [lax.rem(p + o, 4) for o in range(1, 4)] for p in place]

    def ahead(n):
        o = ((0, 2, 1, 3)[n // 16], (n // 4) % 4, n % 4)
        return around[0][o[0]] * 16 + around[1][o[1]] * 4 + around[2][o[2]]

    def behind(n):
        o = ((0, 2, 3, 1)[n // 16], -(n // 4) % 4, -n % 4)
        return around[0][o[0]] * 16 + around[1][o[1]] * 4 + around[2][o[2]]

    def load(n, src, dst):
        return pltpu.make_async_copy(src, dst, load_sem.at[n])

    loads = [
        load(0, cot_in, cot_v),
        load(1, q_in, q_v),
        load(2, k_in, k_v),
        load(3, v_in, v_v),
        load(4, proj_in, proj_v),
        load(5, res_in, res_v),
        load(6, second_in.at[0], second_v.at[pl.ds(0, D)]),
        load(7, first_in.at[0], first_v.at[:, pl.ds(0, D)]),
        load(8, order_in, order_v),
    ]
    for item in loads:
        item.start()

    barrier = pltpu.get_barrier_semaphore()

    for n in range(1, CHIPS):
        pl.semaphore_signal(barrier, inc=1, device_id=(core, ahead(n)), device_id_type=MESH)

    pl.semaphore_signal(barrier, inc=1, device_id=(1 - core, chip), device_id_type=MESH)

    def pair(n, src, dst):
        return pltpu.make_async_remote_copy(
            src, dst, pair_send.at[n], pair_recv.at[n], device_id=(1 - core, chip), device_id_type=MESH
        )

    row_iota = lax.broadcasted_iota(jnp.int32, (MEMBERS * 32, TOK), 0)
    row_of = jnp.where(slot_ref[...] < CAP, route_ref[...] * CAP + slot_ref[...], -1)
    loads[0].wait()
    for m in range(MEMBERS):
        picked = jnp.where(row_iota == row_of[m : m + 1, :], 1.0, 0.0)
        pick_v[m * 128 : (m + 1) * 128, :] = picked.astype(BF16)
        gate_rows = jnp.sum(picked * gates_ref[m : m + 1, :], axis=1, keepdims=True)

        @pl.loop(0, 5)
        def _(n, m=m, gate_rows=gate_rows):
            rows = nn(pick_v[m * 128 : (m + 1) * 128, :], two_lanes(cot_v, n, m)) * gate_rows
            send_a[m * 16 : (m + 1) * 16, :, pl.ds(pl.multiple_of(n * 128, 128), 128)] = pack(rows)

    pl.semaphore_wait(barrier, CHIPS)

    pair_second = pair(0, second_in.at[0], second_v.at[pl.ds(D, D)])
    pair_first = pair(1, first_in.at[0], first_v.at[:, pl.ds(D, D)])
    pair_second.start()
    pair_first.start()

    def dispatch(which, src, dst):
        own = pltpu.make_async_copy(src.at[chip], dst.at[0], local_sem.at[which])
        own.start()

        for n in range(1, CHIPS):
            to = ahead(n)
            pltpu.make_async_remote_copy(
                src.at[to], dst.at[n], a2a_send.at[which], a2a_recv.at[which * 2 + n // 32],
                device_id=(core, to), device_id_type=MESH,
            ).start()

        return own

    def wait_sent(which, ref, count):
        pltpu.make_async_remote_copy(
            ref.at[pl.ds(0, count)], ref.at[pl.ds(0, count)], a2a_send.at[which], a2a_recv.at[which * 2],
            device_id=(1 - core, chip), device_id_type=MESH,
        ).wait_send()

    def wait_landed(n, ref, start, count):
        pltpu.make_async_remote_copy(
            ref.at[pl.ds(start, count)], ref.at[pl.ds(start, count)], a2a_send.at[0], a2a_recv.at[n],
            device_id=(1 - core, chip), device_id_type=MESH,
        ).wait_recv()

    own_grad = dispatch(0, send_a, grad_recv)

    def head_window(h):
        tile = (h * HEAD) // 128
        tile = tile - tile // 9
        lanes = lax.broadcasted_iota(jnp.int32, (1, 256), 1)
        first = h * HEAD - tile * 128
        inside = jnp.where((lanes >= first) & (lanes < first + HEAD), 1.0, 0.0).astype(BF16)
        return pl.ds(pl.multiple_of(tile * 128, 128), 256), inside

    acc_v[0] = jnp.zeros((TOK, D), F32)
    loads[1].wait()
    loads[2].wait()
    loads[3].wait()
    scale = 1.0 / math.sqrt(HEAD)

    @pl.loop(0, HEADS // 4)
    def _(four):
        for one in range(4):
            h = four * 4 + one
            cols, inside = head_window(h)
            scores = nt(q_v[:, cols] * inside, k_v[:, cols]) * scale
            top = jnp.max(scores, axis=1, keepdims=True)
            e = jnp.exp(scores - top)
            weights = e * (1.0 / jnp.sum(e, axis=1, keepdims=True))
            attn_v[h] = weights
            acc_v[0, :, cols] += nn(weights.astype(BF16), v_v[:, cols] * inside)

    @pl.loop(0, 5)
    def _(n):
        cols = pl.ds(pl.multiple_of(n * 256, 256), 256)
        mixed_v[:, cols] = acc_v[0, :, cols].astype(BF16)

    loads[4].wait()
    loads[5].wait()

    @pl.loop(0, 5)
    def _(n):
        cols = pl.ds(pl.multiple_of(n * 256, 256), 256)
        stream = res_v[:, cols].astype(F32) + nn(mixed_v[...], proj_v[:, cols])
        acc_v[2, :, cols] = stream.astype(BF16).astype(F32)

    gain_row = gain_ref[...].reshape(1, D)

    @pl.loop(0, 8)
    def _(b):
        rows = pl.ds(pl.multiple_of(b * 32, 32), 32)
        stream = acc_v[2, rows, :]
        centred = stream - jnp.mean(stream, axis=1, keepdims=True)
        rstd = lax.rsqrt(jnp.mean(centred * centred, axis=1, keepdims=True) + EPS)
        scaled = centred * rstd
        acc_v[2, rows, :] = scaled
        rstd_v[rows, :] = jnp.broadcast_to(rstd, (32, 128))
        enter_v[rows, :] = (scaled * gain_row).astype(BF16)

    @pl.loop(0, 5)
    def _(n):
        rows = nn(pick_v[...], two_lanes(enter_v, n))
        send_b[:, :, pl.ds(pl.multiple_of(n * 128, 128), 128)] = pack(rows)

    own_enter = dispatch(1, send_b, enter_recv)

    pair_mixed = pair(2, mixed_v, mixed_p)
    pair_mixed.start()

    @pl.loop(0, 8)
    def _(b):
        rows = pl.ds(pl.multiple_of(b * 32, 32), 32)
        total = cot_v[0, rows, :].astype(F32)
        for m in range(1, MEMBERS):
            total += cot_v[m, rows, :].astype(F32)
        acc_v[0, rows, :] = total

    def unpack_rows(src, dst, start, count):
        @pl.loop(0, count // 8)
        def _(g):
            chunk = src[pl.ds(start + g * 8, 8)].astype(F32)
            rows = pl.ds(pl.multiple_of(start * 8 + g * 64, 64), 64)
            dst[rows, :HALF] = chunk[:, :CAP, :].reshape(64, HALF).astype(BF16)
            dst[rows, HALF:] = chunk[:, CAP:, :].reshape(64, HALF).astype(BF16)

    own_grad.wait()
    wait_landed(0, grad_recv, 1, 31)
    wait_landed(1, grad_recv, 32, 32)
    unpack_rows(grad_recv, grad_v, 0, CHIPS)
    pair_grad = pair(3, grad_v, grad_p)
    pair_grad.start()
    loads[6].wait()
    pair_second.wait_recv()

    @pl.loop(0, 10)
    def _(t):
        cols = pl.ds(pl.multiple_of(t * 256, 256), 256)
        dpre_v[:, cols] = nt(grad_v[...], second_v[cols, :]).astype(BF16)

    wait_sent(0, send_a, 63)
    loads[7].wait()
    pair_first.wait_recv()

    diagonal = jnp.where(
        lax.broadcasted_iota(jnp.int32, (CAP, 128), 0) == lax.broadcasted_iota(jnp.int32, (CAP, 128), 1), 1.0, 0.0
    )
    pair_enter = []
    for b in range(ROWS // BLOCK):
        chunks = BLOCK // CAP
        if b == 0:
            own_enter.wait()
            wait_landed(2, enter_recv, 1, 31)
        else:
            wait_landed(3, enter_recv, 32, 32)
        unpack_rows(enter_recv, enter_rows, b * chunks, chunks)
        block = pl.ds(b * BLOCK, BLOCK)
        item = pair(4 + b, enter_rows.at[block], enter_p.at[block])
        item.start()
        pair_enter.append(item)
        dot_v[...] = jnp.zeros((BLOCK, 128), F32)

        dot_v[...] = jnp.zeros((BLOCK, 128), F32)

        @pl.loop(0, 10, unroll=2)
        def _(t, block=block):
            cols = pl.ds(pl.multiple_of(t * 256, 256), 256)
            pre = nn(enter_rows[block, :], first_v[:, cols])
            value, slope = gelu_with_grad(pre)
            hidden = value.astype(BF16)
            d_hidden = dpre_v[block, cols].astype(F32)
            hidden_v[block, cols] = hidden
            dpre_v[block, cols] = (slope * d_hidden).astype(BF16)
            both = value * d_hidden
            dot_v[...] += both[:, :128] + both[:, 128:]

        @pl.loop(0, 5)
        def _(n, block=block, b=b, chunks=chunks):
            low = pl.ds(pl.multiple_of(n * 128, 128), 128)
            high = pl.ds(pl.multiple_of(HALF + n * 128, 128), 128)
            weights = jnp.concatenate([first_v[low, :], first_v[high, :]], axis=0)
            send_a[b * chunks : (b + 1) * chunks, :, low] = pack(nt(dpre_v[block, :], weights))

        if b == 0:
            own_back = pltpu.make_async_copy(send_a.at[0], back_recv.at[chip], local_sem.at[2])
            own_back.start()

        for n in range(max(1, b * chunks), (b + 1) * chunks):
            pltpu.make_async_remote_copy(
                send_a.at[n], back_recv.at[chip], a2a_send.at[2], a2a_recv.at[4],
                device_id=(core, behind(n)), device_id_type=MESH,
            ).start()

        dots = jnp.sum(dot_v[...], axis=1, keepdims=True).reshape(chunks, CAP, 1)
        gate_send[b * chunks : (b + 1) * chunks] = jnp.sum(dots * diagonal, axis=1, keepdims=True)

    pair_hidden = pair(6, hidden_v.at[:, pl.ds(D, D)], hidden_p)
    pair_dpre = pair(7, dpre_v.at[:, pl.ds(D, D)], dpre_p)
    pair_hidden.start()
    pair_dpre.start()

    own_gate = pltpu.make_async_copy(gate_send.at[0], gate_recv.at[chip], local_sem.at[3])
    own_gate.start()

    for n in range(1, CHIPS):
        pltpu.make_async_remote_copy(
            gate_send.at[n], gate_recv.at[chip], a2a_send.at[3], a2a_recv.at[5],
            device_id=(core, behind(n)), device_id_type=MESH,
        ).start()

    pair_grad.wait_recv()
    for item in pair_enter:
        item.wait_recv()
    pair_hidden.wait_recv()

    @pl.loop(0, 5)
    def _(t):
        cols = pl.ds(pl.multiple_of(t * 256, 256), 256)
        total = tn(hidden_v[:, cols], grad_v[...]) + tn(hidden_p[:, cols], grad_p[...])
        second_v[cols, :] = total.astype(BF16)

    store_second = pltpu.make_async_copy(second_v.at[pl.ds(0, D)], second_out.at[0], store_sem.at[0])
    store_second.start()
    own_back.wait()
    wait_landed(4, back_recv, 0, 63)

    @pl.loop(0, 5)
    def _(n):
        low = pl.ds(pl.multiple_of(n * 128, 128), 128)
        high = pl.ds(pl.multiple_of(HALF + n * 128, 128), 128)
        chunk = back_recv[:, :, low].astype(F32)
        rows = jnp.concatenate(
            [chunk[:, :CAP, :].reshape(ROWS, 128), chunk[:, CAP:, :].reshape(ROWS, 128)], axis=1
        ).astype(BF16)
        total = tn(pick_v[...], rows)
        acc_v[1, :, low] = total[:, :128]
        acc_v[1, :, high] = total[:, 128:]

    @pl.loop(0, 8)
    def _(b):
        rows = pl.ds(pl.multiple_of(b * 32, 32), 32)
        d_norm = acc_v[1, rows, :]
        scaled = acc_v[2, rows, :]
        by_gain = (d_norm * scaled).astype(BF16)
        d_scaled = d_norm * gain_row
        mean_d = jnp.mean(d_scaled, axis=1, keepdims=True)
        mean_ds = jnp.mean(d_scaled * scaled, axis=1, keepdims=True)
        d_stream = rstd_v[rows, :1] * (d_scaled - mean_d - scaled * mean_ds)
        grad = (acc_v[0, rows, :] + d_stream).astype(BF16)
        resid_v[rows, :] = grad
        for half in range(2):
            rg_v[half, rows, :HALF] = grad[:, half * HALF : (half + 1) * HALF]
            rg_v[half, rows, HALF:] = by_gain[:, half * HALF : (half + 1) * HALF]

    pair_rg = pair(8, rg_v.at[1 - core], rg_p)
    pair_rg.start()
    store_resid = pltpu.make_async_copy(resid_v, resid_out, store_sem.at[2])
    store_resid.start()

    @pl.loop(0, 5)
    def _(n):
        cols = pl.ds(pl.multiple_of(n * 256, 256), 256)
        dmix_v[:, cols] = nt(resid_v[...], proj_v[cols, :]).astype(BF16)

    pair_mixed.wait_recv()
    pair_rg.wait_recv()
    loads[8].wait()
    for n, (order, at) in enumerate(((0, 0), (1, 0), (1, HALF))):
        perm_v[n, 0] = nn(rg_v[core, :, at : at + HALF], order_v[order]).astype(BF16)
        perm_v[n, 1] = nn(rg_p[:, at : at + HALF], order_v[order]).astype(BF16)

    @pl.loop(0, 5)
    def _(t):
        cols = pl.ds(pl.multiple_of(t * 128, 128), 128)
        sum1[0, cols, :] = (
            tn(rg_v[core, :, cols], mixed_v[:, :LANES]) + tn(rg_p[:, cols], mixed_p[:, :LANES])
        ).astype(BF16)
        sum1[1, cols, :] = (
            tn(perm_v[0, 0, :, cols], mixed_v[:, LANES : 2 * LANES])
            + tn(perm_v[0, 1, :, cols], mixed_p[:, LANES : 2 * LANES])
        ).astype(BF16)
        sum1[2, cols, :256] = (
            tn(perm_v[1, 0, :, cols], mixed_v[:, 2 * LANES :]) + tn(perm_v[1, 1, :, cols], mixed_p[:, 2 * LANES :])
        ).astype(BF16)
        ones = jnp.ones((TOK, 256), BF16)
        sum1[2, cols, 256:] = (tn(perm_v[2, 0, :, cols], ones) + tn(perm_v[2, 1, :, cols], ones)).astype(BF16)

    axes = ((0, 1, 2), (1, 0, 2), (2, 0, 1))

    def hop(stage, part, o):
        axis = axes[part][stage]
        to = (place[axis] + o) % 4
        spot = [to if a == axis else place[a] for a in range(3)]
        target = spot[0] * 16 + spot[1] * 4 + spot[2]
        if stage == 0:
            src, dst = sum1.at[part, pl.ds(pl.multiple_of(to * 160, 160), 160)], recv1.at[part, o - 1]
        elif stage == 1:
            src, dst = sum2.at[part, to], recv2.at[part, o - 1]
        else:
            src, dst = sum3.at[part, to], recv3.at[part, o - 1]
        n = (stage * 3 + part) * 3 + o - 1
        return pltpu.make_async_remote_copy(
            src, dst, rs_send.at[n], rs_recv.at[n], device_id=(core, target), device_id_type=MESH
        )

    hops = [[hop(s, p, o) for p in range(3) for o in (1, 3, 2)] for s in range(3)]

    def gathered(stage, part):
        mine = place[axes[part][stage]]
        if stage == 0:
            own, others = sum1[part, pl.ds(pl.multiple_of(mine * 160, 160), 160), :], recv1
        elif stage == 1:
            own, others = sum2[part, mine], recv2
        else:
            own, others = sum3[part, mine], recv3
        total = own.astype(F32)
        for o in range(3):
            total += others[part, o].astype(F32)
        return total

    for item in hops[0]:
        item.start()

    pair_dpre.wait_recv()

    @pl.loop(0, 5)
    def _(t):
        cols = pl.ds(pl.multiple_of(t * 256, 256), 256)
        total = tn(enter_rows[:, cols], dpre_v[:, :D]) + tn(enter_p[:, cols], dpre_p[...])
        first_v[cols, :D] = total.astype(BF16)

    store_first = pltpu.make_async_copy(first_v.at[:, pl.ds(0, D)], first_out.at[0], store_sem.at[1])
    store_first.start()

    acc_v[...] = jnp.zeros((3, TOK, D), F32)

    def attention_back(start, stop):
        @pl.loop(start, stop)
        def _(four):
            for one in range(4):
                h = four * 4 + one
                cols, inside = head_window(h)
                d_mixed = dmix_v[:, cols] * inside
                weights = attn_v[h]
                d_weights = nt(d_mixed, v_v[:, cols])
                shift = jnp.sum(d_weights * weights, axis=1, keepdims=True)
                d_scores = (weights * (d_weights - shift) * scale).astype(BF16)
                acc_v[0, :, cols] += nn(d_scores, k_v[:, cols] * inside)
                acc_v[1, :, cols] += tn(d_scores, q_v[:, cols] * inside)
                acc_v[2, :, cols] += tn(weights.astype(BF16), d_mixed)

    attention_back(0, 2)
    for item in hops[0]:
        item.wait_recv()
    for part in range(3):
        total = gathered(0, part)
        for t in range(4):
            sum2[part, t] = jnp.concatenate([total[t * 40 : (t + 1) * 40], jnp.zeros((8, LANES), F32)], axis=0).astype(BF16)
    for item in hops[1]:
        item.start()

    attention_back(2, 3)
    for item in hops[1]:
        item.wait_recv()
    row = lax.broadcasted_iota(jnp.int32, (16, 48), 0)
    col = lax.broadcasted_iota(jnp.int32, (16, 48), 1)
    for part in range(3):
        total = gathered(1, part).astype(BF16)
        for t in range(4):
            chosen = jnp.where((col == row + SHARE * t) & (row < SHARE), 1.0, 0.0).astype(BF16)
            sum3[part, t] = nn(chosen, total).astype(BF16)
    for item in hops[2]:
        item.start()

    attention_back(3, 4)
    stores = []
    for n, (staged, out) in enumerate(((q_v, q_out), (k_v, k_out), (v_v, v_out))):

        @pl.loop(0, 5)
        def _(t, n=n, staged=staged):
            cols = pl.ds(pl.multiple_of(t * 256, 256), 256)
            staged[:, cols] = acc_v[n, :, cols].astype(BF16)

        item = pltpu.make_async_copy(staged, out, store_sem.at[3 + n])
        item.start()
        stores.append(item)

    own_gate.wait()
    wait_landed(5, gate_recv, 0, 63)
    for m in range(MEMBERS):
        dots = gate_recv[m * 16 : (m + 1) * 16] * diagonal
        dots = jnp.sum(dots, axis=2, keepdims=True).reshape(128, 1)
        total = jnp.sum(pick_v[m * 128 : (m + 1) * 128, :].astype(F32) * dots, axis=0, keepdims=True)
        gate_out[m : m + 1, :] = total / gates_ref[m : m + 1, :]

    for item in hops[2]:
        item.wait_recv()
    for part in range(3):
        share_out[:, part * LANES : (part + 1) * LANES] = gathered(2, part)

    for stage in hops:
        for item in stage:
            item.wait_send()
    wait_sent(1, send_b, 63)
    wait_sent(2, send_a, 63)
    wait_sent(3, gate_send, 63)
    for item in (pair_second, pair_first, pair_mixed, pair_grad, *pair_enter, pair_hidden, pair_dpre, pair_rg):
        item.wait_send()
    for item in (store_second, store_first, store_resid, *stores):
        item.wait()


def finish(
    resid_in, q_in, k_in, v_in, first_in, second_in, share_ref, gate_ref,
    resid_out, q_out, k_out, v_out, first_out, second_out, proj_out, gain_out, gate_out,
    wide_v, rows_v, sem,
):
    pieces = [
        (first_in.at[0, pl.ds(0, HALF)], first_out.at[0, pl.ds(0, HALF)], wide_v.at[0, 0]),
        (second_in.at[0, pl.ds(0, HALF)], second_out.at[0, pl.ds(0, HALF)], wide_v.at[1, 0]),
        (first_in.at[0, pl.ds(HALF, HALF)], first_out.at[0, pl.ds(HALF, HALF)], wide_v.at[0, 1]),
        (second_in.at[0, pl.ds(HALF, HALF)], second_out.at[0, pl.ds(HALF, HALF)], wide_v.at[1, 1]),
        (resid_in, resid_out, rows_v.at[0]),
        (q_in, q_out, rows_v.at[1]),
        (k_in, k_out, rows_v.at[2]),
        (v_in, v_out, rows_v.at[3]),
    ]
    loads = [pltpu.make_async_copy(src, held, sem.at[0, n]) for n, (src, _, held) in enumerate(pieces)]
    stores = [pltpu.make_async_copy(held, dst, sem.at[1, n]) for n, (_, dst, held) in enumerate(pieces)]
    for item in loads:
        item.start()
    for load, store in zip(loads, stores):
        load.wait()
        store.start()
    proj_out[...] = share_ref[:SHARE, :D]
    row = lax.broadcasted_iota(jnp.int32, (16, 128), 0)
    col = lax.broadcasted_iota(jnp.int32, (16, 128), 1)
    gain = jnp.sum(jnp.where(row == col, share_ref[:, D : D + 128], 0.0), axis=0, keepdims=True)
    gain_out[...] = gain[:, :SHARE]
    gate_out[...] = gate_ref[...]
    for item in stores:
        item.wait()


def shards(queries, keys_in, values_in, resid, out_proj, ln_gain, w_in, w_out, route, slot, gates, cotangent):
    any_spec = pl.BlockSpec(memory_space=pl.ANY)
    vmem_spec = pl.BlockSpec(memory_space=pltpu.VMEM)
    order = jnp.asarray(block_orders(), BF16)
    tokens = jax.ShapeDtypeStruct((TOK, D), BF16)
    square = jax.ShapeDtypeStruct((1, D, D), BF16)
    bf = lambda *shape: pltpu.VMEM(shape, BF16)
    fl = lambda *shape: pltpu.VMEM(shape, F32)
    dma = lambda n: pltpu.SemaphoreType.DMA((n,))
    resid_grad, query_grad, key_grad, value_grad, share, gate_grad, first_grad, second_grad = pl.pallas_call(
        kernel,
        out_shape=(
            tokens, tokens, tokens, tokens,
            jax.ShapeDtypeStruct((16, 3 * LANES), F32),
            jax.ShapeDtypeStruct((MEMBERS, TOK), F32),
            square, square,
        ),
        in_specs=[any_spec] * 5 + [vmem_spec] + [any_spec] * 2 + [vmem_spec] * 3 + [any_spec] * 2,
        out_specs=(any_spec,) * 4 + (vmem_spec,) * 2 + (any_spec,) * 2,
        scratch_shapes=[
            bf(TOK, D), bf(TOK, D), bf(TOK, D), bf(TOK, D), bf(D, D), bf(MEMBERS, TOK, D), bf(2, HALF, HALF),
            bf(D, H), bf(H, D),
            fl(HEADS, TOK, TOK), fl(3, TOK, D), bf(TOK, D), bf(TOK, D), fl(TOK, 128), bf(TOK, D), bf(ROWS, TOK),
            bf(CHIPS, 16, HALF), bf(CHIPS, 16, HALF), bf(CHIPS, 16, HALF), bf(CHIPS, 16, HALF), bf(CHIPS, 16, HALF),
            bf(ROWS, D), bf(ROWS, D), bf(ROWS, D), bf(ROWS, D), bf(ROWS, H), bf(ROWS, H), bf(ROWS, D), bf(ROWS, D),
            fl(BLOCK, 128),
            bf(2, TOK, D), bf(TOK, D), bf(3, 2, TOK, HALF), bf(TOK, D), bf(TOK, D),
            fl(CHIPS, 1, 128), fl(CHIPS, 1, 128),
            bf(3, HALF, LANES), bf(3, 3, 160, LANES), bf(3, 4, 48, LANES), bf(3, 3, 48, LANES),
            bf(3, 4, 16, LANES), bf(3, 3, 16, LANES),
            dma(9), dma(6), dma(4), dma(9), dma(9), dma(4), dma(6), dma(27), dma(27),
        ],
        compiler_params=pltpu.CompilerParams(
            collective_id=0, has_side_effects=True, vmem_limit_bytes=63 * 1024 * 1024
        ),
        cost_estimate=pl.CostEstimate(flops=25_000_000_000, bytes_accessed=40_000_000, transcendentals=4_000_000),
    )(queries, keys_in, values_in, resid, out_proj, ln_gain, w_in, w_out, route, slot, gates, cotangent, order)
    resid_grad, query_grad, key_grad, value_grad, first_grad, second_grad, proj_grad, gain_grad, gate_grad = pl.pallas_call(
        finish,
        out_shape=(
            tokens, tokens, tokens, tokens, square, square,
            jax.ShapeDtypeStruct((SHARE, D), F32),
            jax.ShapeDtypeStruct((1, SHARE), F32),
            jax.ShapeDtypeStruct((MEMBERS, TOK), F32),
        ),
        in_specs=[any_spec] * 6 + [vmem_spec] * 2,
        out_specs=(any_spec,) * 6 + (vmem_spec,) * 3,
        scratch_shapes=[bf(2, 2, HALF, D), bf(4, TOK, D), pltpu.SemaphoreType.DMA((2, 8))],
        compiler_params=pltpu.CompilerParams(vmem_limit_bytes=60 * 1024 * 1024),
    )(resid_grad, query_grad, key_grad, value_grad, first_grad, second_grad, share, gate_grad)
    return (
        resid_grad, query_grad, key_grad, value_grad, proj_grad.T, gain_grad.reshape(SHARE), gate_grad,
        first_grad, second_grad,
    )


def solution(mesh):
    both = ("dp", "expert")
    return jax.shard_map(
        shards,
        mesh=mesh,
        in_specs=(
            P(both, None), P(both, None), P(both, None), P(both, None), P(), P(),
            P("expert", None, "dp"), P("expert", "dp", None),
            P(None, both), P(None, both), P(None, both), P(None, both, None),
        ),
        out_specs=(
            P(both, None), P(both, None), P(both, None), P(both, None), P(None, both), P(both), P(None, both),
            P("expert", None, "dp"), P("expert", "dp", None),
        ),
        check_vma=False,
    )
```
